512 devices in a mesh: inp: 2 (over core), chan: 8 (over y), tgrp: 32 (over z, x).
Axes of the slice: x: 4, y: 8, z: 8, core: 2. Of those that a mesh axis runs over, the one named last changes fastest.
Arguments:
- voltages: bfloat16 [2048, 524288], P(('inp', 'chan'), 'tgrp'), may hold values from -6 to 6
- input_flags: int32 [2048, 1024], P(('inp', 'chan')), may hold values 0 or 1
- channel_to_slot: int32 [1024], replicated, may hold values from -1 to 31, as said below
Outputs:
- visibility: float32 [32, 64, 2, 32, 1088], P('chan', ('inp', 'tgrp'))
The draws below stay inside these ranges and needn't reach their ends.
Inputs may be any that keep to these rules, and one draw needn't show every extreme that they name: `channel_to_slot`: no slot is named by two channels. Frequency owner o holds the slots o * 4 to (o + 1) * 4 - 1 and receives between 1 and 4 channels, which fill its lowest slots; the last owner always receives 4 channels. Channels named -1 are not correlated.
All inputs are finite; a program needn't handle non-finite values. No bound on the sum of `input_flags` on one device may be relied on, other than what follows from the above.
Results may differ from the reference program's by a relative error of at most 0.0058.
Values may be sent and summed in bfloat16 or wider, within the bound.
No kernel may reach another device: no remote copies, remote signals or barrier semaphores. Data moves between devices by JAX's collectives and lax.ppermute only.
A program may use at most 64 MiB of HBM per device.

```python
import math
import jax
import jax.numpy as jnp
import numpy as np
from jax import lax

INPUT_COUNT = 2048
FRAME_SAMPLES = 2048
NCHAN = 1024
TAPS = 4
OWNER_SLOTS = 4
NBLK = 64
BLK = 32
KT = 34
SLOT_TOTAL = 32
FRAME_TOTAL = 256


def draw_channel_to_slot(key, part):
    key = jax.random.fold_in(key, 7)
    key_count, key_full, key_perm = jax.random.split(key, 3)
    frequency_owner_list = SLOT_TOTAL // OWNER_SLOTS
    counts = jax.random.randint(key_count, (frequency_owner_list,), 1, OWNER_SLOTS + 1)
    fullest = jax.random.randint(key_full, (), 0, frequency_owner_list)
    owner_numbers = jnp.arange(frequency_owner_list)
    counts = jnp.where((owner_numbers == fullest) | (owner_numbers == frequency_owner_list - 1), OWNER_SLOTS, counts)
    slot_numbers = jnp.arange(SLOT_TOTAL, dtype=jnp.int32)
    slot_used = slot_numbers % OWNER_SLOTS < counts[slot_numbers // OWNER_SLOTS]
    slot_rank = jnp.cumsum(slot_used.astype(jnp.int32)) - 1
    channel_order = jax.random.permutation(key_perm, NCHAN)
    target = jnp.where(slot_used, channel_order[jnp.clip(slot_rank, 0, NCHAN - 1)], NCHAN)
    table_out = jnp.full((NCHAN + 1,), -1, jnp.int32).at[target].set(slot_numbers)
    return table_out[:NCHAN]


def touch_ends(drawn, stream_key, low, top_value):
    longest = drawn.shape.index(max(drawn.shape))
    spots = []
    for shift in (0, 1):
        where = [jax.random.randint(jax.random.fold_in(stream_key, axis), (), 0, length) for axis, length in enumerate(drawn.shape)]
        where[longest] = (where[longest] + shift) % drawn.shape[longest]
        spots.append(tuple(where))
    return drawn.at[spots[0]].set(low).at[spots[1]].set(top_value)


def block_levels(stream_key, shape, cuts, least, largest):
    factor_of, own = 1.0, jax.random.fold_in(stream_key, 6)
    for position, blocks in cuts:
        draws = jnp.exp(jax.random.uniform(jax.random.fold_in(own, position), (blocks,), jnp.float32, least / len(cuts), largest / len(cuts)))
        factor_of = factor_of * jnp.repeat(draws, shape[position] // blocks).reshape([-1 if axis == position else 1 for axis in range(len(shape))])
    return factor_of


def centred(rng, extent, spread, most, pieces=(), kind=jnp.bfloat16):
    result = spread * jax.random.normal(rng, extent, jnp.float32)
    if pieces:
        result = result * block_levels(rng, extent, pieces, -0.22, 0.18)
    return jnp.clip(result, -most, most).astype(kind)


def setup_inputs(seed: int = 0) -> dict:
    keys = jax.random.split(jax.random.key(seed), 4)
    voltages = centred(keys[0], (INPUT_COUNT, FRAME_TOTAL * FRAME_SAMPLES), 1.0, 6.0, ((0, 16), (1, 32)))
    input_flags = touch_ends((jax.random.randint(keys[1], (INPUT_COUNT, NCHAN), 0, 10) < 9).astype(jnp.int32), jax.random.fold_in(keys[1], 1), 0, 1)
    channel_to_slot = draw_channel_to_slot(jax.random.fold_in(keys[3], 71), 0)
    return {"voltages": voltages, "input_flags": input_flags, "channel_to_slot": channel_to_slot}


def window_table():
    sample = jnp.arange(TAPS * FRAME_SAMPLES, dtype=jnp.float32)
    middle = (sample + 0.5 - 0.5 * TAPS * FRAME_SAMPLES) / FRAME_SAMPLES
    hanning = 0.5 - 0.5 * jnp.cos(2.0 * math.pi * (sample + 0.5) / (TAPS * FRAME_SAMPLES))
    return (jnp.sinc(middle) * hanning).reshape(TAPS, FRAME_SAMPLES)

def slot_lookup_tables(channel_to_slot, slot_count):
    slot_numbers = jnp.arange(slot_count, dtype=jnp.int32)
    chan_ids = jnp.arange(NCHAN, dtype=jnp.int32)
    labelled_items = channel_to_slot[:, None] == slot_numbers[None, :]
    slot_channel = lax.optimization_barrier(jnp.sum(jnp.where(labelled_items, chan_ids[:, None], 0), 0)).astype(jnp.int32)
    slot_used = jnp.any(labelled_items, 0)
    sample = jnp.arange(FRAME_SAMPLES, dtype=jnp.int32)
    phase_angle = (slot_channel[:, None] * sample[None, :] % FRAME_SAMPLES).astype(jnp.float32) * (2.0 * math.pi / FRAME_SAMPLES)
    cosine_matrix = jnp.where(slot_used[:, None], jnp.cos(phase_angle), 0.0).astype(jnp.bfloat16)
    sine_matrix = jnp.where(slot_used[:, None], -jnp.sin(phase_angle), 0.0).astype(jnp.bfloat16)
    return (labelled_items, cosine_matrix, sine_matrix)

def filter_frames(padded, window_taps, frame_count):
    summed = window_taps[0] * padded[:, 0:frame_count, :].astype(jnp.float32)
    for offset in range(1, TAPS):
        summed = summed + window_taps[offset] * padded[:, offset:offset + frame_count, :].astype(jnp.float32)
    return summed.astype(jnp.bfloat16)

def reference(voltages, input_flags, channel_to_slot):
    window_taps = window_table()
    labelled_items, cosine_matrix, sine_matrix = slot_lookup_tables(channel_to_slot, SLOT_TOTAL)
    dft_table = jnp.concatenate([cosine_matrix, sine_matrix], 0).astype(jnp.float32)
    flagged_choice = jnp.dot(input_flags.astype(jnp.float32), labelled_items.astype(jnp.float32), precision=lax.Precision.HIGHEST)
    grouped_row_list = min(16, INPUT_COUNT)

    def spectrum_block_part(block_args):
        voltage_rows, flagged_row_list = block_args
        frames = voltage_rows.reshape(grouped_row_list, FRAME_TOTAL, FRAME_SAMPLES)
        padded = jnp.concatenate([jnp.zeros((grouped_row_list, TAPS - 1, FRAME_SAMPLES), frames.dtype), frames], 1)
        filtered = filter_frames(padded, window_taps, FRAME_TOTAL)
        channel_spectra = jnp.einsum('cm,ifm->icf', dft_table, filtered.astype(jnp.float32), precision=lax.Precision.HIGHEST) * 0.03125
        channel_spectra = channel_spectra.reshape(grouped_row_list, 2, SLOT_TOTAL, FRAME_TOTAL) * flagged_row_list[:, None, :, None]
        return channel_spectra.astype(jnp.bfloat16)
    slot_placed = lax.map(spectrum_block_part, (voltages.reshape(INPUT_COUNT // grouped_row_list, grouped_row_list, FRAME_TOTAL * FRAME_SAMPLES), flagged_choice.reshape(INPUT_COUNT // grouped_row_list, grouped_row_list, SLOT_TOTAL)))
    slot_placed = jnp.transpose(slot_placed.reshape(INPUT_COUNT, 2, SLOT_TOTAL, FRAME_TOTAL), (2, 0, 1, 3))
    rows_index = np.arange(NBLK)[:, None] + np.zeros((1, KT), np.int32)
    cols_index = (np.arange(NBLK)[:, None] + np.arange(KT)[None, :] - 1) % NBLK
    norm_scale = 1.0 / math.sqrt(FRAME_TOTAL)

    def slot_visibility(channel_spectra):
        real_part = channel_spectra[:, 0]
        imag_part = channel_spectra[:, 1]
        right_rows = jnp.concatenate([real_part, imag_part], 1)
        left_rows = jnp.concatenate([right_rows, jnp.concatenate([imag_part, -real_part], 1)], 0)
        products = jnp.dot(left_rows, right_rows.T, preferred_element_type=jnp.float32) * norm_scale
        blocks = products.reshape(2, NBLK, BLK, NBLK, BLK)
        picked = blocks[:, rows_index, :, cols_index, :]
        return jnp.transpose(picked, (0, 2, 3, 1, 4)).reshape(NBLK, 2, BLK, KT * BLK)
    return lax.map(slot_visibility, slot_placed)
```

```python
import math

import jax
import jax.numpy as jnp
import numpy as np
from jax import lax
from jax.experimental import pallas as pl
from jax.experimental.pallas import tpu as pltpu
from jax.sharding import Mesh, PartitionSpec as P

FRAME_SAMPLES = 2048
NCHAN = 1024
TAPS = 4
SLOTS = 32
FRAMES = 8
IN_DEV = 128
LANES = 128
BLK = 32
KT = 34
ROW_TARGETS = 4
GATHER = 8
MESSAGE = 2 * FRAMES
SPECTRUM_SCALE = 2.0**-7
NT = (((1,), (1,)), ((), ()))
VMEM = pltpu.VMEM


def window_table():
    sample = np.arange(TAPS * FRAME_SAMPLES, dtype=np.float64)
    middle = (sample + 0.5 - 0.5 * TAPS * FRAME_SAMPLES) / FRAME_SAMPLES
    hanning = 0.5 - 0.5 * np.cos(2.0 * math.pi * (sample + 0.5) / (TAPS * FRAME_SAMPLES))
    return (np.sinc(middle) * hanning).reshape(TAPS, FRAME_SAMPLES).astype(np.float32)


def spectra_kernel(slots_ref, window_ref, flags_hbm, volts_hbm, spec_ref, part_ref, kept_ref, volts, table, flags, sems):
    copies = []
    for frame in range(FRAMES):
        copy = pltpu.make_async_copy(
            volts_hbm.at[:, pl.ds(frame * FRAME_SAMPLES, FRAME_SAMPLES)],
            volts.at[frame // 2, pl.ds(frame % 2 * IN_DEV, IN_DEV), :],
            sems.at[frame],
        )
        copy.start()
        copies.append(copy)
    flag_copy = pltpu.make_async_copy(flags_hbm, flags, sems.at[FRAMES])
    flag_copy.start()

    chosen = lax.broadcasted_iota(jnp.int32, (SLOTS, NCHAN), 0) == slots_ref[...]
    channel = jnp.sum(
        jnp.where(chosen, lax.broadcasted_iota(jnp.int32, (SLOTS, NCHAN), 1), 0).astype(jnp.float32), 1, keepdims=True
    ).astype(jnp.int32)
    lane = lax.broadcasted_iota(jnp.int32, (SLOTS, LANES), 1)
    turn = 2.0 * math.pi / FRAME_SAMPLES
    fine = ((channel * lane) & (FRAME_SAMPLES - 1)).astype(jnp.float32) * turn
    coarse = ((channel * (lane * LANES)) & (FRAME_SAMPLES - 1)).astype(jnp.float32) * turn
    fine_cos, fine_sin = jnp.cos(fine), jnp.sin(fine)
    coarse_cos, coarse_sin = jnp.cos(coarse), jnp.sin(coarse)
    for piece in range(FRAME_SAMPLES // LANES):
        at = pl.ds(piece * LANES, LANES)
        ccos, csin = coarse_cos[:, piece : piece + 1], coarse_sin[:, piece : piece + 1]
        cosine = (ccos * fine_cos - csin * fine_sin).astype(jnp.bfloat16).astype(jnp.float32)
        sine = (-(csin * fine_cos + ccos * fine_sin)).astype(jnp.bfloat16).astype(jnp.float32)
        for tap in range(TAPS):
            weight = window_ref[tap : tap + 1, at]
            table[pl.ds(tap * 64, 32), at] = (cosine * weight).astype(jnp.bfloat16)
            table[pl.ds(tap * 64 + 32, 32), at] = (sine * weight).astype(jnp.bfloat16)

    flag_copy.wait()
    kept_ref[...] = lax.dot_general(
        chosen.astype(jnp.float32).astype(jnp.bfloat16),
        flags[...].astype(jnp.float32).astype(jnp.bfloat16),
        NT,
        preferred_element_type=jnp.float32,
    )

    sums = {}
    for pair in range(FRAMES // 2):
        copies[2 * pair].wait()
        copies[2 * pair + 1].wait()
        terms = lax.dot_general(table[...], volts[pair], NT, preferred_element_type=jnp.float32)
        for half in range(2):
            for tap in range(TAPS):
                frame = 2 * pair + half + TAPS - 1 - tap
                term = terms[tap * 64 : tap * 64 + 64, half * IN_DEV : (half + 1) * IN_DEV]
                sums[frame] = term if frame not in sums else sums[frame] + term
        for frame in [f for f in sums if f < 2 * pair + 2]:
            done = sums.pop(frame)
            spec_ref[frame] = done[:32]
            spec_ref[FRAMES + frame] = done[32:]
    for frame, done in sums.items():
        part_ref[frame - FRAMES] = done[:32]
        part_ref[TAPS - 1 + frame - FRAMES] = done[32:]


def slotted_kernel(spec_ref, part_ref, kept_ref, out_ref, rows):
    kept = kept_ref[...]
    for frame in range(FRAMES):
        for half in range(2):
            value = spec_ref[half * FRAMES + frame]
            if frame < TAPS - 1:
                value = value + part_ref[half * (TAPS - 1) + frame]
            rows[pl.ds(half * FRAMES + frame, SLOTS, stride=MESSAGE), :] = value * kept
    out_ref[...] = rows[...].astype(jnp.bfloat16)


def product_kernel(place_ref, own_ref, other_ref, out_ref, left, prod):
    zl, x = place_ref[0], place_ref[1]
    depth = GATHER * 64
    pick = (
        lax.broadcasted_iota(jnp.int32, (BLK, LANES), 1) == lax.broadcasted_iota(jnp.int32, (BLK, LANES), 0) + BLK * x
    ).astype(jnp.float32).astype(jnp.bfloat16)
    for target in range(ROW_TARGETS):
        rows = own_ref[:, 2 * target + zl, :, :].reshape(depth, LANES)
        wide = rows.astype(jnp.float32).reshape(depth // MESSAGE, MESSAGE, LANES)
        turned = jnp.concatenate([wide[:, FRAMES:], -wide[:, :FRAMES]], 1).reshape(depth, LANES).astype(jnp.bfloat16)
        left[pl.ds(target * 64, BLK), :] = lax.dot_general(
            pick, rows, NT, preferred_element_type=jnp.float32
        ).astype(jnp.bfloat16)
        left[pl.ds(target * 64 + BLK, BLK), :] = lax.dot_general(
            pick, turned, NT, preferred_element_type=jnp.float32
        ).astype(jnp.bfloat16)
    for source, ref in enumerate((own_ref, other_ref)):
        for pair in range(4):
            right = jnp.concatenate(
                [ref[:, 2 * pair + i, :, :].reshape(depth, LANES) for i in range(2)], 1
            )
            value = jnp.dot(left[...], right, preferred_element_type=jnp.float32)
            group = source * 8 + pair * 2
            prod[:, pl.ds((group + 1) * LANES, 2 * LANES)] = value
            if group == 0:
                prod[:, pl.ds(17 * LANES, LANES)] = value[:, :LANES]
            if group == 14:
                prod[:, pl.ds(0, LANES)] = value[:, LANES:]
    first = zl + jnp.where(x == 0, 0, 1)
    shift = lax.rem(x + 3, 4) * BLK
    span = 10 * LANES
    for target in range(ROW_TARGETS):
        start = pl.multiple_of((first + 2 * target) * LANES, LANES)
        window = prod[pl.ds(target * 64, 64), pl.ds(start, span)]
        window = pltpu.roll(window, lax.rem(span - shift, span), 1)
        out_ref[target] = window[:, : KT * BLK].astype(jnp.bfloat16)


def on_device(voltages, input_flags, channel_to_slot):
    any_space = pl.BlockSpec(memory_space=pl.ANY)
    vmem = pl.BlockSpec(memory_space=VMEM)
    f32, bf16 = jnp.float32, jnp.bfloat16
    window = jnp.asarray(window_table() * np.float32(SPECTRUM_SCALE))
    spec, part, kept = pl.pallas_call(
        spectra_kernel,
        out_shape=(
            jax.ShapeDtypeStruct((MESSAGE, SLOTS, IN_DEV), f32),
            jax.ShapeDtypeStruct((2 * (TAPS - 1), SLOTS, IN_DEV), f32),
            jax.ShapeDtypeStruct((SLOTS, IN_DEV), f32),
        ),
        in_specs=[vmem, vmem, any_space, any_space],
        out_specs=(vmem, vmem, vmem),
        scratch_shapes=[
            VMEM((FRAMES // 2, 2 * IN_DEV, FRAME_SAMPLES), bf16),
            VMEM((TAPS * 64, FRAME_SAMPLES), bf16),
            VMEM((IN_DEV, NCHAN), jnp.int32),
            pltpu.SemaphoreType.DMA((FRAMES + 1,)),
        ],
        compiler_params=pltpu.CompilerParams(vmem_limit_bytes=24 * 2**20),
        name="spectra",
    )(channel_to_slot[None, :], window, input_flags, voltages)

    groups = [(i, i + 1) for i in range(31)]
    history = lax.ppermute(part, ("zh", "zl", "x"), groups)

    slotted = pl.pallas_call(
        slotted_kernel,
        out_shape=jax.ShapeDtypeStruct((SLOTS * MESSAGE, IN_DEV), bf16),
        in_specs=[vmem, vmem, vmem],
        out_specs=vmem,
        scratch_shapes=[VMEM((SLOTS * MESSAGE, IN_DEV), f32)],
        name="slotted",
    )(spec, history, kept)

    placed = lax.all_to_all(
        slotted.reshape(SLOTS, MESSAGE, IN_DEV), ("chan", "zh"), split_axis=0, concat_axis=0, tiled=True
    )
    copies = jnp.broadcast_to(placed.reshape(1, SLOTS * MESSAGE, IN_DEV), (GATHER, SLOTS * MESSAGE, IN_DEV))
    own = lax.all_to_all(copies, ("zl", "x"), split_axis=0, concat_axis=0, tiled=True)
    other = lax.ppermute(own, "inp", [(0, 1), (1, 0)])

    place = jnp.stack([lax.axis_index("zl"), lax.axis_index("x")]).astype(jnp.int32)
    blocked = (GATHER, 8, 64, LANES)
    rows = pl.pallas_call(
        product_kernel,
        out_shape=jax.ShapeDtypeStruct((ROW_TARGETS, 64, KT * BLK), bf16),
        in_specs=[pl.BlockSpec(memory_space=pltpu.SMEM), vmem, vmem],
        out_specs=vmem,
        scratch_shapes=[VMEM((256, GATHER * 64), bf16), VMEM((256, 18 * LANES), f32)],
        compiler_params=pltpu.CompilerParams(vmem_limit_bytes=24 * 2**20),
        name="products",
    )(place, own.reshape(blocked), other.reshape(blocked))

    tiles = lax.all_to_all(rows, "zh", split_axis=0, concat_axis=0, tiled=True)
    return tiles.astype(f32).reshape(ROW_TARGETS, 1, 2, BLK, KT * BLK)


def solution(mesh):
    parts = Mesh(mesh.devices.reshape(2, 8, 4, 2, 4), ("inp", "chan", "zh", "zl", "x"))
    return jax.shard_map(
        on_device,
        mesh=parts,
        in_specs=(P(("inp", "chan"), ("zh", "zl", "x")), P(("inp", "chan"), None), P()),
        out_specs=P("chan", ("inp", "zh", "zl", "x"), None, None, None),
        check_vma=False,
    )
```

```python
import math

import jax
import jax.numpy as jnp
import numpy as np
from jax import lax
from jax.experimental import pallas as pl
from jax.experimental.pallas import tpu as pltpu
from jax.sharding import Mesh, PartitionSpec as P

FRAME_SAMPLES = 2048
NCHAN = 1024
TAPS = 4
SLOTS = 32
FRAMES = 8
IN_DEV = 128
LANES = 128
BLK = 32
KT = 34
OWNER_SLOTS = 4
GROUPS = 8
HELD = 5
MESSAGE = 24
SLICE = 72
CARRY = TAPS - 1
SPECTRUM_SCALE = 2.0**-7
NT = (((1,), (1,)), ((), ()))
VMEM = pltpu.VMEM


def window_table():
    sample = np.arange(TAPS * FRAME_SAMPLES, dtype=np.float64)
    middle = (sample + 0.5 - 0.5 * TAPS * FRAME_SAMPLES) / FRAME_SAMPLES
    hanning = 0.5 - 0.5 * np.cos(2.0 * math.pi * (sample + 0.5) / (TAPS * FRAME_SAMPLES))
    return (np.sinc(middle) * hanning).reshape(TAPS, FRAME_SAMPLES).astype(np.float32)


def spectra_kernel(
    slots_hbm, window_hbm, flags_hbm, volts_hbm, out_ref, slots, window, volts, table, flags, rows, sems
):
    small = []
    for index, (source, target) in enumerate(((slots_hbm, slots), (window_hbm, window), (flags_hbm, flags))):
        small.append(pltpu.make_async_copy(source, target, sems.at[FRAMES + index]))
        small[-1].start()
    copies = []
    for frame in range(FRAMES):
        copy = pltpu.make_async_copy(
            volts_hbm.at[:, pl.ds(frame * FRAME_SAMPLES, FRAME_SAMPLES)],
            volts.at[frame // 2, pl.ds(frame % 2 * IN_DEV, IN_DEV), :],
            sems.at[frame],
        )
        copy.start()
        copies.append(copy)

    small[0].wait()
    chosen = lax.broadcasted_iota(jnp.int32, (SLOTS, NCHAN), 0) == slots[...]
    channel = jnp.sum(
        jnp.where(chosen, lax.broadcasted_iota(jnp.int32, (SLOTS, NCHAN), 1), 0).astype(jnp.float32), 1, keepdims=True
    ).astype(jnp.int32)
    lane = lax.broadcasted_iota(jnp.int32, (SLOTS, LANES), 1)
    turn = 2.0 * math.pi / FRAME_SAMPLES
    fine = ((channel * lane) & (FRAME_SAMPLES - 1)).astype(jnp.float32) * turn
    coarse = ((channel * (lane * LANES)) & (FRAME_SAMPLES - 1)).astype(jnp.float32) * turn
    fine_cos, fine_sin = jnp.cos(fine), jnp.sin(fine)
    coarse_cos, coarse_sin = jnp.cos(coarse), jnp.sin(coarse)
    small[1].wait()
    for piece in range(FRAME_SAMPLES // LANES):
        at = pl.ds(piece * LANES, LANES)
        ccos, csin = coarse_cos[:, piece : piece + 1], coarse_sin[:, piece : piece + 1]
        cosine = (ccos * fine_cos - csin * fine_sin).astype(jnp.bfloat16).astype(jnp.float32)
        sine = (-(csin * fine_cos + ccos * fine_sin)).astype(jnp.bfloat16).astype(jnp.float32)
        for tap in range(TAPS):
            weight = window[tap : tap + 1, at]
            table[pl.ds(tap * 64, 32), at] = (cosine * weight).astype(jnp.bfloat16)
            table[pl.ds(tap * 64 + 32, 32), at] = (sine * weight).astype(jnp.bfloat16)

    small[2].wait()
    kept = lax.dot_general(
        chosen.astype(jnp.float32).astype(jnp.bfloat16),
        flags[...].astype(jnp.float32).astype(jnp.bfloat16),
        NT,
        preferred_element_type=jnp.float32,
    )

    sums = {}
    for pair in range(FRAMES // 2):
        copies[2 * pair].wait()
        copies[2 * pair + 1].wait()
        terms = lax.dot_general(table[...], volts[pair], NT, preferred_element_type=jnp.float32)
        for half in range(2):
            for tap in range(TAPS):
                frame = 2 * pair + half + TAPS - 1 - tap
                term = terms[tap * 64 : tap * 64 + 64, half * IN_DEV : (half + 1) * IN_DEV]
                sums[frame] = term if frame not in sums else sums[frame] + term
        for frame in [f for f in sums if f < 2 * pair + 2]:
            done = sums.pop(frame)
            rows[pl.ds(frame, SLOTS, stride=MESSAGE), :] = done[:32] * kept
            rows[pl.ds(FRAMES + frame, SLOTS, stride=MESSAGE), :] = done[32:] * kept
    empty = jnp.zeros((SLOTS, LANES), jnp.float32)
    for frame in range(CARRY + 1):
        real, imag = (sums[FRAMES + frame][:32] * kept, sums[FRAMES + frame][32:] * kept) if frame < CARRY else (empty, empty)
        rows[pl.ds(2 * FRAMES + frame, SLOTS, stride=MESSAGE), :] = real
        rows[pl.ds(2 * FRAMES + 4 + frame, SLOTS, stride=MESSAGE), :] = imag
    out_ref[...] = rows[...].reshape(SLOTS, MESSAGE, LANES).astype(jnp.bfloat16)


def with_carry(real, imag, carried):
    axis = real.ndim - 2
    early = lax.broadcasted_iota(jnp.int32, real.shape, axis) < CARRY
    return real + jnp.where(early, carried, 0.0), imag + jnp.where(early, pltpu.roll(carried, 4, axis), 0.0)


def pack_kernel(in_ref, out_ref):
    slices = []
    for group in range(GROUPS):
        pieces, carried = [], None
        for source in range(4):
            message = in_ref[4 * group + source].astype(jnp.float32)
            real, imag = message[:8], message[8:16]
            if source:
                real, imag = with_carry(real, imag, carried)
            pieces += [real, imag]
            carried = message[16:]
        slices.append(jnp.concatenate(pieces + [carried], 0).astype(jnp.bfloat16))
    for target in range(GROUPS):
        parity = target % 2
        taken = [parity + 2 * i for i in range(4)] + [target + 1 - 2 * parity]
        for place, group in enumerate(taken):
            out_ref[target, place] = slices[group]


def joined(ref, place):
    wide = ref[:, place].astype(jnp.float32)
    carried = jnp.concatenate([jnp.zeros((1, 8, LANES), jnp.float32), wide[: GROUPS - 1, 64:]], 0)
    real, imag = with_carry(wide[:, :8], wide[:, 8:16], carried)
    return jnp.concatenate([real, imag, wide[:, 16:64]], 1).reshape(GROUPS * 64, LANES)


def columns(ref, pair):
    return jnp.concatenate([joined(ref, 2 * pair + i).astype(jnp.bfloat16) for i in range(2)], 1)


def own_kernel(place_ref, own_ref, left_ref, prod_ref):
    same = lax.broadcasted_iota(jnp.int32, (LANES, LANES), 0) == lax.broadcasted_iota(jnp.int32, (LANES, LANES), 1)
    same = same.astype(jnp.float32).astype(jnp.bfloat16)
    depth = GROUPS * 64
    for kind, place in enumerate((place_ref[0], HELD - 1)):
        wide = joined(own_ref, place)
        split = wide.reshape(depth // 16, 16, LANES)
        turned = jnp.concatenate([split[:, 8:], -split[:, :8]], 1).reshape(depth, LANES)
        for half, value in enumerate((wide, turned)):
            left_ref[pl.ds(kind * 256 + half * LANES, LANES), :] = lax.dot_general(
                same, value.astype(jnp.bfloat16), NT, preferred_element_type=jnp.float32
            ).astype(jnp.bfloat16)
    for pair in range(2):
        prod_ref[:, pl.ds(pair * 256, 256)] = jnp.dot(
            left_ref[...], columns(own_ref, pair), preferred_element_type=jnp.float32
        )


def other_kernel(place_ref, left_ref, prod_ref, other_ref, out_ref, ring):
    zh, zl = place_ref[0], place_ref[1]
    ring[:, pl.ds(LANES, 4 * LANES)] = prod_ref[...]
    ring[:, pl.ds(9 * LANES, LANES)] = prod_ref[:, :LANES]
    for pair in range(2):
        value = jnp.dot(left_ref[...], columns(other_ref, pair), preferred_element_type=jnp.float32)
        ring[:, pl.ds((5 + 2 * pair) * LANES, 2 * LANES)] = value
        if pair == 1:
            ring[:, pl.ds(0, LANES)] = value[:, LANES:]
    for kind in range(2):
        target = (zl if kind == 0 else 1 - zl) * 4
        for x in range(4):
            first = zh if kind == 0 else zh - zl + (1 if x else 0)
            start = pl.multiple_of((first + 1) * LANES, LANES)
            for half in range(2):
                row = kind * 256 + half * LANES + x * BLK
                out_ref[target + x, pl.ds(half * BLK, BLK), :] = ring[
                    pl.ds(row, BLK), pl.ds(start, 5 * LANES)
                ].astype(jnp.bfloat16)


def tiles_kernel(place_ref, in_ref, out_ref):
    zl, x, slot = place_ref[1], place_ref[2], pl.program_id(0)
    even = lax.rem(zl + jnp.where(x == 0, 1, 0), 2)
    sides = [in_ref[even * 4 + slot], in_ref[(1 - even) * 4 + slot]]
    pieces = [sides[k % 2][:, k // 2 * LANES : (k // 2 + 1) * LANES] for k in range(10)]
    window = jnp.concatenate(pieces, 1).astype(jnp.float32)
    span = 10 * LANES
    window = pltpu.roll(window, span - lax.rem(x + 3, 4) * BLK, 1)
    out_ref[0] = window[:, : KT * BLK]


def on_device(voltages, input_flags, channel_to_slot):
    hbm = pl.BlockSpec(memory_space=pltpu.HBM)
    vmem = pl.BlockSpec(memory_space=VMEM)
    smem = pl.BlockSpec(memory_space=pltpu.SMEM)
    f32, bf16 = jnp.float32, jnp.bfloat16
    limit = lambda mib: pltpu.CompilerParams(vmem_limit_bytes=mib * 2**20)
    window = jnp.asarray(window_table() * np.float32(SPECTRUM_SCALE))
    place = jnp.stack([lax.axis_index("zh"), lax.axis_index("zl"), lax.axis_index("x")]).astype(jnp.int32)
    slotted = pl.pallas_call(
        spectra_kernel,
        out_shape=jax.ShapeDtypeStruct((SLOTS, MESSAGE, LANES), bf16),
        in_specs=[hbm, hbm, hbm, hbm],
        out_specs=vmem,
        scratch_shapes=[
            VMEM((1, NCHAN), jnp.int32),
            VMEM((TAPS, FRAME_SAMPLES), f32),
            VMEM((FRAMES // 2, 2 * IN_DEV, FRAME_SAMPLES), bf16),
            VMEM((TAPS * 64, FRAME_SAMPLES), bf16),
            VMEM((IN_DEV, NCHAN), jnp.int32),
            VMEM((SLOTS * MESSAGE, LANES), f32),
            pltpu.SemaphoreType.DMA((FRAMES + 3,)),
        ],
        compiler_params=limit(60),
        name="spectra",
    )(channel_to_slot[None, :], window, input_flags, voltages)
    placed = lax.all_to_all(slotted, ("chan", "x"), split_axis=0, concat_axis=0, tiled=True)
    packed = pl.pallas_call(
        pack_kernel,
        out_shape=jax.ShapeDtypeStruct((GROUPS, HELD, SLICE, LANES), bf16),
        in_specs=[vmem],
        out_specs=vmem,
        compiler_params=limit(8),
        name="pack",
    )(placed)
    own = lax.all_to_all(packed, ("zh", "zl"), split_axis=0, concat_axis=0, tiled=True)
    other = lax.ppermute(own, "inp", [(0, 1), (1, 0)])
    depth = GROUPS * 64
    left, prod = pl.pallas_call(
        own_kernel,
        out_shape=(jax.ShapeDtypeStruct((512, depth), bf16), jax.ShapeDtypeStruct((512, 4 * LANES), f32)),
        in_specs=[smem, vmem],
        out_specs=(vmem, vmem),
        compiler_params=limit(8),
        cost_estimate=pl.CostEstimate(flops=2 * 512 * 512 * 512, bytes_accessed=3 * 2**20, transcendentals=0),
        name="own",
    )(place, own)
    rows = pl.pallas_call(
        other_kernel,
        out_shape=jax.ShapeDtypeStruct((8, 64, 5 * LANES), bf16),
        in_specs=[smem, vmem, vmem, vmem],
        out_specs=vmem,
        scratch_shapes=[VMEM((512, 10 * LANES), f32)],
        compiler_params=limit(12),
        name="other",
    )(place, left, prod, other)
    parts = lax.all_to_all(rows, ("zl", "x"), split_axis=0, concat_axis=0, tiled=True)
    tiles = pl.pallas_call(
        tiles_kernel,
        grid=(OWNER_SLOTS,),
        out_shape=jax.ShapeDtypeStruct((OWNER_SLOTS, 64, KT * BLK), f32),
        in_specs=[smem, vmem],
        out_specs=pl.BlockSpec((1, 64, KT * BLK), lambda slot: (slot, 0, 0)),
        compiler_params=limit(8),
        name="tiles",
    )(place, parts)
    return tiles.reshape(OWNER_SLOTS, 1, 2, BLK, KT * BLK)


def solution(mesh):
    parts = Mesh(mesh.devices.reshape(2, 8, 4, 2, 4), ("inp", "chan", "zh", "zl", "x"))
    return jax.shard_map(
        on_device,
        mesh=parts,
        in_specs=(P(("inp", "chan"), ("zh", "zl", "x")), P(("inp", "chan"), None), P()),
        out_specs=P("chan", ("inp", "zh", "zl", "x"), None, None, None),
        check_vma=False,
    )
```

```python
import math

import jax
import jax.numpy as jnp
import numpy as np
from jax import lax
from jax.experimental import pallas as pl
from jax.experimental.pallas import tpu as pltpu
from jax.sharding import Mesh, PartitionSpec as P

FRAME_SAMPLES = 2048
NCHAN = 1024
TAPS = 4
SLOTS = 32
FRAMES = 8
IN_DEV = 128
LANES = 128
BLK = 32
KT = 34
OWNER_SLOTS = 4
GROUPS = 8
HELD = 5
MESSAGE = 24
SLICE = 72
CARRY = TAPS - 1
SPECTRUM_SCALE = 2.0**-7
NT = (((1,), (1,)), ((), ()))
VMEM = pltpu.VMEM


def window_table():
    sample = np.arange(TAPS * FRAME_SAMPLES, dtype=np.float64)
    middle = (sample + 0.5 - 0.5 * TAPS * FRAME_SAMPLES) / FRAME_SAMPLES
    hanning = 0.5 - 0.5 * np.cos(2.0 * math.pi * (sample + 0.5) / (TAPS * FRAME_SAMPLES))
    return (np.sinc(middle) * hanning).reshape(TAPS, FRAME_SAMPLES).astype(np.float32)


def spectra_kernel(
    slots_hbm, window_hbm, flags_hbm, volts_hbm, out_ref, slots, window, volts, table, flags, rows, sems
):
    small = []
    for index, (source, target) in enumerate(((slots_hbm, slots), (window_hbm, window), (flags_hbm, flags))):
        small.append(pltpu.make_async_copy(source, target, sems.at[FRAMES + index]))
        small[-1].start()
    copies = []
    for frame in range(FRAMES):
        copy = pltpu.make_async_copy(
            volts_hbm.at[:, pl.ds(frame * FRAME_SAMPLES, FRAME_SAMPLES)],
            volts.at[frame // 2, pl.ds(frame % 2 * IN_DEV, IN_DEV), :],
            sems.at[frame],
        )
        copy.start()
        copies.append(copy)

    small[0].wait()
    chosen = lax.broadcasted_iota(jnp.int32, (SLOTS, NCHAN), 0) == slots[...]
    channel = jnp.sum(
        jnp.where(chosen, lax.broadcasted_iota(jnp.int32, (SLOTS, NCHAN), 1), 0).astype(jnp.float32), 1, keepdims=True
    ).astype(jnp.int32)
    lane = lax.broadcasted_iota(jnp.int32, (SLOTS, LANES), 1)
    turn = 2.0 * math.pi / FRAME_SAMPLES
    fine = ((channel * lane) & (FRAME_SAMPLES - 1)).astype(jnp.float32) * turn
    coarse = ((channel * (lane * LANES)) & (FRAME_SAMPLES - 1)).astype(jnp.float32) * turn
    fine_cos, fine_sin = jnp.cos(fine), jnp.sin(fine)
    coarse_cos, coarse_sin = jnp.cos(coarse), jnp.sin(coarse)
    small[1].wait()
    for piece in range(FRAME_SAMPLES // LANES):
        at = pl.ds(piece * LANES, LANES)
        ccos, csin = coarse_cos[:, piece : piece + 1], coarse_sin[:, piece : piece + 1]
        cosine = (ccos * fine_cos - csin * fine_sin).astype(jnp.bfloat16).astype(jnp.float32)
        sine = (-(csin * fine_cos + ccos * fine_sin)).astype(jnp.bfloat16).astype(jnp.float32)
        for tap in range(TAPS):
            weight = window[tap : tap + 1, at]
            table[pl.ds(tap * 64, 32), at] = (cosine * weight).astype(jnp.bfloat16)
            table[pl.ds(tap * 64 + 32, 32), at] = (sine * weight).astype(jnp.bfloat16)

    small[2].wait()
    kept = lax.dot_general(
        chosen.astype(jnp.float32).astype(jnp.bfloat16),
        flags[...].astype(jnp.float32).astype(jnp.bfloat16),
        NT,
        preferred_element_type=jnp.float32,
    )

    sums = {}
    for pair in range(FRAMES // 2):
        if pair % 2 == 0:
            for copy in copies[2 * pair : 2 * pair + 4]:
                copy.wait()
        terms = lax.dot_general(table[...], volts[pair], NT, preferred_element_type=jnp.float32)
        for half in range(2):
            for tap in range(TAPS):
                frame = 2 * pair + half + TAPS - 1 - tap
                term = terms[tap * 64 : tap * 64 + 64, half * IN_DEV : (half + 1) * IN_DEV]
                sums[frame] = term if frame not in sums else sums[frame] + term
        for frame in [f for f in sums if f < 2 * pair + 2]:
            done = sums.pop(frame)
            rows[pl.ds(frame, SLOTS, stride=MESSAGE), :] = done[:32] * kept
            rows[pl.ds(FRAMES + frame, SLOTS, stride=MESSAGE), :] = done[32:] * kept
    empty = jnp.zeros((SLOTS, LANES), jnp.float32)
    for frame in range(CARRY + 1):
        real, imag = (sums[FRAMES + frame][:32] * kept, sums[FRAMES + frame][32:] * kept) if frame < CARRY else (empty, empty)
        rows[pl.ds(2 * FRAMES + frame, SLOTS, stride=MESSAGE), :] = real
        rows[pl.ds(2 * FRAMES + 4 + frame, SLOTS, stride=MESSAGE), :] = imag
    out_ref[...] = rows[...].reshape(SLOTS, MESSAGE, LANES).astype(jnp.bfloat16)


def with_carry(real, imag, carried):
    axis = real.ndim - 2
    early = lax.broadcasted_iota(jnp.int32, real.shape, axis) < CARRY
    return real + jnp.where(early, carried, 0.0), imag + jnp.where(early, pltpu.roll(carried, 4, axis), 0.0)


def pack_kernel(in_ref, out_ref):
    slices = []
    for group in range(GROUPS):
        pieces, carried = [], None
        for source in range(4):
            message = in_ref[4 * group + source].astype(jnp.float32)
            real, imag = message[:8], message[8:16]
            if source:
                real, imag = with_carry(real, imag, carried)
            pieces += [real, imag]
            carried = message[16:]
        slices.append(jnp.concatenate(pieces + [carried], 0).astype(jnp.bfloat16))
    for target in range(GROUPS):
        parity = target % 2
        taken = [parity + 2 * i for i in range(4)] + [target + 1 - 2 * parity]
        for place, group in enumerate(taken):
            out_ref[target, place] = slices[group]


def joined(ref, place):
    wide = ref[:, place].astype(jnp.float32)
    carried = jnp.concatenate([jnp.zeros((1, 8, LANES), jnp.float32), wide[: GROUPS - 1, 64:]], 0)
    real, imag = with_carry(wide[:, :8], wide[:, 8:16], carried)
    return jnp.concatenate([real, imag, wide[:, 16:64]], 1).reshape(GROUPS * 64, LANES)


def columns(ref, pair):
    return jnp.concatenate([joined(ref, 2 * pair + i).astype(jnp.bfloat16) for i in range(2)], 1)


def own_kernel(own_ref, left_ref, prod_ref):
    same = lax.broadcasted_iota(jnp.int32, (LANES, LANES), 0) == lax.broadcasted_iota(jnp.int32, (LANES, LANES), 1)
    same = same.astype(jnp.float32).astype(jnp.bfloat16)
    depth = GROUPS * 64
    for kind, place in enumerate((lax.axis_index("zh"), HELD - 1)):
        wide = joined(own_ref, place)
        split = wide.reshape(depth // 16, 16, LANES)
        turned = jnp.concatenate([split[:, 8:], -split[:, :8]], 1).reshape(depth, LANES)
        for half, value in enumerate((wide, turned)):
            left_ref[pl.ds(kind * 256 + half * LANES, LANES), :] = lax.dot_general(
                same, value.astype(jnp.bfloat16), NT, preferred_element_type=jnp.float32
            ).astype(jnp.bfloat16)
    for pair in range(2):
        prod_ref[:, pl.ds(pair * 256, 256)] = jnp.dot(
            left_ref[...], columns(own_ref, pair), preferred_element_type=jnp.float32
        )


def other_kernel(left_ref, prod_ref, other_ref, out_ref, ring):
    zh, zl = lax.axis_index("zh"), lax.axis_index("zl")
    ring[:, pl.ds(LANES, 4 * LANES)] = prod_ref[...]
    ring[:, pl.ds(9 * LANES, LANES)] = prod_ref[:, :LANES]
    for pair in range(2):
        value = jnp.dot(left_ref[...], columns(other_ref, pair), preferred_element_type=jnp.float32)
        ring[:, pl.ds((5 + 2 * pair) * LANES, 2 * LANES)] = value
        if pair == 1:
            ring[:, pl.ds(0, LANES)] = value[:, LANES:]
    for kind in range(2):
        target = (zl if kind == 0 else 1 - zl) * 4
        for x in range(4):
            first = zh if kind == 0 else zh - zl + (1 if x else 0)
            start = pl.multiple_of((first + 1) * LANES, LANES)
            for half in range(2):
                row = kind * 256 + half * LANES + x * BLK
                out_ref[target + x, pl.ds(half * BLK, BLK), :] = ring[
                    pl.ds(row, BLK), pl.ds(start, 5 * LANES)
                ].astype(jnp.bfloat16)


def tiles_kernel(in_ref, out_hbm, tiles, sems):
    zl, x = lax.axis_index("zl"), lax.axis_index("x")
    even = lax.rem(zl + jnp.where(x == 0, 1, 0), 2)
    span = 10 * LANES
    shift = span - lax.rem(x + 3, 4) * BLK
    copies = []
    for slot in range(OWNER_SLOTS):
        sides = [in_ref[even * 4 + slot], in_ref[(1 - even) * 4 + slot]]
        pieces = [sides[k % 2][:, k // 2 * LANES : (k // 2 + 1) * LANES] for k in range(10)]
        window = pltpu.roll(jnp.concatenate(pieces, 1).astype(jnp.float32), shift, 1)
        tiles[slot] = window[:, : KT * BLK]
        copies.append(pltpu.make_async_copy(tiles.at[slot], out_hbm.at[slot], sems.at[slot]))
        copies[-1].start()
    for copy in copies:
        copy.wait()


def on_device(voltages, input_flags, channel_to_slot):
    hbm = pl.BlockSpec(memory_space=pltpu.HBM)
    vmem = pl.BlockSpec(memory_space=VMEM)
    f32, bf16 = jnp.float32, jnp.bfloat16
    limit = lambda mib: pltpu.CompilerParams(vmem_limit_bytes=mib * 2**20)
    in_hbm = lambda value: pltpu.with_memory_space_constraint(value, pltpu.HBM)
    window = jnp.asarray(window_table() * np.float32(SPECTRUM_SCALE))
    slotted = pl.pallas_call(
        spectra_kernel,
        out_shape=VMEM((SLOTS, MESSAGE, LANES), bf16),
        in_specs=[hbm, hbm, hbm, hbm],
        out_specs=vmem,
        scratch_shapes=[
            VMEM((1, NCHAN), jnp.int32),
            VMEM((TAPS, FRAME_SAMPLES), f32),
            VMEM((FRAMES // 2, 2 * IN_DEV, FRAME_SAMPLES), bf16),
            VMEM((TAPS * 64, FRAME_SAMPLES), bf16),
            VMEM((IN_DEV, NCHAN), jnp.int32),
            VMEM((SLOTS * MESSAGE, LANES), f32),
            pltpu.SemaphoreType.DMA((FRAMES + 3,)),
        ],
        compiler_params=limit(16),
        name="spectra",
    )(*(in_hbm(value) for value in (channel_to_slot[None, :], window, input_flags, voltages)))
    placed = lax.all_to_all(slotted, ("chan", "x"), split_axis=0, concat_axis=0, tiled=True)
    packed = pl.pallas_call(
        pack_kernel,
        out_shape=jax.ShapeDtypeStruct((GROUPS, HELD, SLICE, LANES), bf16),
        in_specs=[vmem],
        out_specs=vmem,
        compiler_params=limit(8),
        name="pack",
    )(placed)
    own = lax.all_to_all(packed, ("zh", "zl"), split_axis=0, concat_axis=0, tiled=True)
    other = lax.ppermute(own, "inp", [(0, 1), (1, 0)])
    depth = GROUPS * 64
    left, prod = pl.pallas_call(
        own_kernel,
        out_shape=(jax.ShapeDtypeStruct((512, depth), bf16), jax.ShapeDtypeStruct((512, 4 * LANES), f32)),
        in_specs=[vmem],
        out_specs=(vmem, vmem),
        compiler_params=limit(8),
        cost_estimate=pl.CostEstimate(flops=2 * 512 * 512 * 512, bytes_accessed=3 * 2**20, transcendentals=0),
        name="own",
    )(own)
    rows = pl.pallas_call(
        other_kernel,
        out_shape=jax.ShapeDtypeStruct((8, 64, 5 * LANES), bf16),
        in_specs=[vmem, vmem, vmem],
        out_specs=vmem,
        scratch_shapes=[VMEM((512, 10 * LANES), f32)],
        compiler_params=limit(12),
        name="other",
    )(left, prod, other)
    parts = lax.all_to_all(rows, ("zl", "x"), split_axis=0, concat_axis=0, tiled=True)
    tiles = pl.pallas_call(
        tiles_kernel,
        out_shape=jax.ShapeDtypeStruct((OWNER_SLOTS, 64, KT * BLK), f32),
        in_specs=[vmem],
        out_specs=hbm,
        scratch_shapes=[VMEM((OWNER_SLOTS, 64, KT * BLK), f32), pltpu.SemaphoreType.DMA((OWNER_SLOTS,))],
        compiler_params=limit(8),
        name="tiles",
    )(parts)
    return tiles.reshape(OWNER_SLOTS, 1, 2, BLK, KT * BLK)


def solution(mesh):
    parts = Mesh(mesh.devices.reshape(2, 8, 4, 2, 4), ("inp", "chan", "zh", "zl", "x"))
    return jax.shard_map(
        on_device,
        mesh=parts,
        in_specs=(P(("inp", "chan"), ("zh", "zl", "x")), P(("inp", "chan"), None), P()),
        out_specs=P("chan", ("inp", "zh", "zl", "x"), None, None, None),
        check_vma=False,
    )
```

```python
import math

import jax
import jax.numpy as jnp
import numpy as np
from jax import lax
from jax.experimental import pallas as pl
from jax.experimental.pallas import tpu as pltpu
from jax.sharding import Mesh, PartitionSpec as P

FRAME_SAMPLES = 2048
NCHAN = 1024
TAPS = 4
SLOTS = 32
FRAMES = 8
IN_DEV = 128
LANES = 128
BLK = 32
KT = 34
OWNER_SLOTS = 4
GROUPS = 8
HELD = 5
MESSAGE = 24
SLICE = 64
BUNDLE = HELD * SLICE + 32
CUT = 18 * BLK
PARCEL = 4 * 64 + 32
CARRY = TAPS - 1
SPECTRUM_SCALE = 2.0**-7
NT = (((1,), (1,)), ((), ()))
VMEM = pltpu.VMEM


def window_table():
    sample = np.arange(TAPS * FRAME_SAMPLES, dtype=np.float64)
    middle = (sample + 0.5 - 0.5 * TAPS * FRAME_SAMPLES) / FRAME_SAMPLES
    hanning = 0.5 - 0.5 * np.cos(2.0 * math.pi * (sample + 0.5) / (TAPS * FRAME_SAMPLES))
    return (np.sinc(middle) * hanning).reshape(TAPS, FRAME_SAMPLES).astype(np.float32)


def spectra_kernel(
    slots_hbm, window_hbm, flags_hbm, volts_hbm, out_ref, slots, window, volts, table, flags, rows, sems
):
    small = []
    for index, (source, target) in enumerate(((slots_hbm, slots), (window_hbm, window), (flags_hbm, flags))):
        small.append(pltpu.make_async_copy(source, target, sems.at[FRAMES + index]))
        small[-1].start()
    copies = []
    for frame in range(FRAMES):
        copy = pltpu.make_async_copy(
            volts_hbm.at[:, pl.ds(frame * FRAME_SAMPLES, FRAME_SAMPLES)],
            volts.at[frame // 2, pl.ds(frame % 2 * IN_DEV, IN_DEV), :],
            sems.at[frame],
        )
        copy.start()
        copies.append(copy)

    small[0].wait()
    chosen = lax.broadcasted_iota(jnp.int32, (SLOTS, NCHAN), 0) == slots[...]
    channel = jnp.sum(
        jnp.where(chosen, lax.broadcasted_iota(jnp.int32, (SLOTS, NCHAN), 1), 0).astype(jnp.float32), 1, keepdims=True
    ).astype(jnp.int32)
    lane = lax.broadcasted_iota(jnp.int32, (SLOTS, LANES), 1)
    turn = 2.0 * math.pi / FRAME_SAMPLES
    fine = ((channel * lane) & (FRAME_SAMPLES - 1)).astype(jnp.float32) * turn
    coarse = ((channel * (lane * LANES)) & (FRAME_SAMPLES - 1)).astype(jnp.float32) * turn
    fine_cos, fine_sin = jnp.cos(fine), jnp.sin(fine)
    coarse_cos, coarse_sin = jnp.cos(coarse), jnp.sin(coarse)
    small[1].wait()
    for piece in range(FRAME_SAMPLES // LANES):
        at = pl.ds(piece * LANES, LANES)
        ccos, csin = coarse_cos[:, piece : piece + 1], coarse_sin[:, piece : piece + 1]
        cosine = (ccos * fine_cos - csin * fine_sin).astype(jnp.bfloat16).astype(jnp.float32)
        sine = (-(csin * fine_cos + ccos * fine_sin)).astype(jnp.bfloat16).astype(jnp.float32)
        for tap in range(TAPS):
            weight = window[tap : tap + 1, at]
            table[pl.ds(tap * 64, 32), at] = (cosine * weight).astype(jnp.bfloat16)
            table[pl.ds(tap * 64 + 32, 32), at] = (sine * weight).astype(jnp.bfloat16)

    small[2].wait()
    kept = lax.dot_general(
        chosen.astype(jnp.float32).astype(jnp.bfloat16),
        flags[...].astype(jnp.float32).astype(jnp.bfloat16),
        NT,
        preferred_element_type=jnp.float32,
    )

    sums = {}
    for pair in range(FRAMES // 2):
        if pair % 2 == 0:
            for copy in copies[2 * pair : 2 * pair + 4]:
                copy.wait()
        terms = lax.dot_general(table[...], volts[pair], NT, preferred_element_type=jnp.float32)
        for half in range(2):
            for tap in range(TAPS):
                frame = 2 * pair + half + TAPS - 1 - tap
                term = terms[tap * 64 : tap * 64 + 64, half * IN_DEV : (half + 1) * IN_DEV]
                sums[frame] = term if frame not in sums else sums[frame] + term
        for frame in [f for f in sums if f < 2 * pair + 2]:
            done = sums.pop(frame)
            rows[pl.ds(frame, SLOTS, stride=MESSAGE), :] = done[:32] * kept
            rows[pl.ds(FRAMES + frame, SLOTS, stride=MESSAGE), :] = done[32:] * kept
    empty = jnp.zeros((SLOTS, LANES), jnp.float32)
    for frame in range(CARRY + 1):
        real, imag = (sums[FRAMES + frame][:32] * kept, sums[FRAMES + frame][32:] * kept) if frame < CARRY else (empty, empty)
        rows[pl.ds(2 * FRAMES + frame, SLOTS, stride=MESSAGE), :] = real
        rows[pl.ds(2 * FRAMES + 4 + frame, SLOTS, stride=MESSAGE), :] = imag
    out_ref[...] = rows[...].reshape(SLOTS, MESSAGE, LANES).astype(jnp.bfloat16)


def with_carry(real, imag, carried):
    axis = real.ndim - 2
    early = lax.broadcasted_iota(jnp.int32, real.shape, axis) < CARRY
    return real + jnp.where(early, carried, 0.0), imag + jnp.where(early, pltpu.roll(carried, 4, axis), 0.0)


def pack_kernel(in_ref, out_ref):
    slices, sums = [], []
    for group in range(GROUPS):
        pieces, carried = [], None
        for source in range(4):
            message = in_ref[4 * group + source].astype(jnp.float32)
            real, imag = message[:8], message[8:16]
            if source:
                real, imag = with_carry(real, imag, carried)
            pieces += [real, imag]
            carried = message[16:]
        slices.append(jnp.concatenate(pieces, 0).astype(jnp.bfloat16))
        sums.append(carried)
    unused = lax.broadcasted_iota(jnp.int32, (8, LANES), 0) % 4 == CARRY
    for target in range(GROUPS):
        parity = target % 2
        extra = target + 1 - 2 * parity
        taken = [parity + 2 * i for i in range(4)]
        for place, group in enumerate(taken + [extra]):
            out_ref[target, pl.ds(place * SLICE, SLICE), :] = slices[group]
        last = [
            jnp.where(unused, pltpu.roll(sums[extra], CARRY - i, 0), sums[group]) if i < CARRY else sums[group]
            for i, group in enumerate(taken)
        ]
        out_ref[target, pl.ds(HELD * SLICE, 32), :] = jnp.concatenate(last, 0).astype(jnp.bfloat16)


def joined(ref, place):
    start = place * SLICE if isinstance(place, int) else pl.multiple_of(place * SLICE, SLICE)
    wide = ref[:, pl.ds(start, SLICE), :].astype(jnp.float32)
    sums = ref[: GROUPS - 1, pl.ds(HELD * SLICE, 32), :].astype(jnp.float32)
    sums = [sums[:, 8 * i : 8 * i + 8] for i in range(4)]
    if not isinstance(place, int):
        carried = sum(jnp.where(place == i, sums[i], 0.0) for i in range(4))
    elif place < 4:
        carried = sums[place]
    else:
        row = lax.broadcasted_iota(jnp.int32, sums[0].shape, 1) % 4
        carried = sum(jnp.where(row == i, pltpu.roll(sums[i], 5 + i, 1), 0.0) for i in range(CARRY))
    carried = jnp.concatenate([jnp.zeros((1, 8, LANES), jnp.float32), carried], 0)
    real, imag = with_carry(wide[:, :8], wide[:, 8:16], carried)
    return jnp.concatenate([real, imag, wide[:, 16:]], 1).reshape(GROUPS * SLICE, LANES)


def columns(ref, pair):
    return jnp.concatenate([joined(ref, 2 * pair + i).astype(jnp.bfloat16) for i in range(2)], 1)


def own_kernel(own_ref, left_ref, prod_ref):
    same = lax.broadcasted_iota(jnp.int32, (LANES, LANES), 0) == lax.broadcasted_iota(jnp.int32, (LANES, LANES), 1)
    same = same.astype(jnp.float32).astype(jnp.bfloat16)
    depth = GROUPS * 64
    for kind, place in enumerate((lax.axis_index("zh"), HELD - 1)):
        wide = joined(own_ref, place)
        split = wide.reshape(depth // 16, 16, LANES)
        turned = jnp.concatenate([split[:, 8:], -split[:, :8]], 1).reshape(depth, LANES)
        for half, value in enumerate((wide, turned)):
            left_ref[pl.ds(kind * 256 + half * LANES, LANES), :] = lax.dot_general(
                same, value.astype(jnp.bfloat16), NT, preferred_element_type=jnp.float32
            ).astype(jnp.bfloat16)
    for pair in range(2):
        prod_ref[:, pl.ds(pair * 256, 256)] = jnp.dot(
            left_ref[...], columns(own_ref, pair), preferred_element_type=jnp.float32
        )


def other_kernel(left_ref, prod_ref, other_ref, out_ref, ring):
    zh, zl = lax.axis_index("zh"), lax.axis_index("zl")
    ring[:, pl.ds(LANES, 4 * LANES)] = prod_ref[...]
    ring[:, pl.ds(9 * LANES, LANES)] = prod_ref[:, :LANES]
    for pair in range(2):
        value = jnp.dot(left_ref[...], columns(other_ref, pair), preferred_element_type=jnp.float32)
        ring[:, pl.ds((5 + 2 * pair) * LANES, 2 * LANES)] = value
        if pair == 1:
            ring[:, pl.ds(0, LANES)] = value[:, LANES:]
    lane = lax.broadcasted_iota(jnp.int32, (BLK, LANES), 1)
    for kind in range(2):
        target = (zl if kind == 0 else 1 - zl) * 4
        for x in range(4):
            first = zh if kind == 0 else zh - zl + (1 if x else 0)
            start = pl.multiple_of((first + 1) * LANES, LANES)
            skipped = (x + 3) % 4 * BLK
            leads = (kind == 0) == (x > 0)
            lasts = []
            for half in range(2):
                value = ring[pl.ds(kind * 256 + half * LANES + x * BLK, BLK), pl.ds(start, 5 * LANES)]
                groups = [value[:, i * LANES : (i + 1) * LANES] for i in range(5)]
                if skipped:
                    groups = [pltpu.roll(group, LANES - skipped, 1) for group in groups]
                lasts.append(groups[4][:, : LANES // 2])
                if leads and skipped:
                    groups[0] = jnp.where(lane < LANES - skipped, groups[0], groups[4])
                for tile in range(4):
                    out_ref[target + x, pl.ds(tile * 64 + half * BLK, BLK), :] = groups[tile].astype(jnp.bfloat16)
            out_ref[target + x, pl.ds(256, BLK), :] = jnp.concatenate(lasts, 1).astype(jnp.bfloat16)


def tiles_kernel(in_ref, out_hbm, tiles, sems):
    zl, x = lax.axis_index("zl"), lax.axis_index("x")
    leading = lax.rem(zl + jnp.where(x == 0, 1, 0), 2)
    first = lax.broadcasted_iota(jnp.int32, (64, LANES), 1) < LANES - lax.rem(x + 3, 4) * BLK
    copies = []
    for slot in range(OWNER_SLOTS):
        sides = []
        for parity in (leading, 1 - leading):
            wide = in_ref[parity * 4 + slot].astype(jnp.float32)
            last = wide[256:]
            sides.append([wide[64 * i : 64 * i + 64] for i in range(4)] + [
                jnp.concatenate([last, pltpu.roll(last, LANES // 2, 1)], 0)
            ])
        even, odd = sides
        for i in range(4):
            tiles[slot, :, pl.ds(2 * i * LANES, LANES)] = jnp.where(first, even[i], odd[i])
            tiles[slot, :, pl.ds((2 * i + 1) * LANES, LANES)] = jnp.where(first, odd[i], even[(i + 1) % 4])
        tiles[slot, :, pl.ds(8 * LANES, LANES // 2)] = jnp.where(first, even[4], odd[4])[:, : LANES // 2]
        copies.append(pltpu.make_async_copy(tiles.at[slot], out_hbm.at[slot], sems.at[slot]))
        copies[-1].start()
    for copy in copies:
        copy.wait()


def on_device(voltages, input_flags, channel_to_slot):
    hbm = pl.BlockSpec(memory_space=pltpu.HBM)
    vmem = pl.BlockSpec(memory_space=VMEM)
    f32, bf16 = jnp.float32, jnp.bfloat16
    limit = lambda mib: pltpu.CompilerParams(vmem_limit_bytes=mib * 2**20)
    in_hbm = lambda value: pltpu.with_memory_space_constraint(value, pltpu.HBM)
    window = jnp.asarray(window_table() * np.float32(SPECTRUM_SCALE))
    slotted = pl.pallas_call(
        spectra_kernel,
        out_shape=VMEM((SLOTS, MESSAGE, LANES), bf16),
        in_specs=[hbm, hbm, hbm, hbm],
        out_specs=vmem,
        scratch_shapes=[
            VMEM((1, NCHAN), jnp.int32),
            VMEM((TAPS, FRAME_SAMPLES), f32),
            VMEM((FRAMES // 2, 2 * IN_DEV, FRAME_SAMPLES), bf16),
            VMEM((TAPS * 64, FRAME_SAMPLES), bf16),
            VMEM((IN_DEV, NCHAN), jnp.int32),
            VMEM((SLOTS * MESSAGE, LANES), f32),
            pltpu.SemaphoreType.DMA((FRAMES + 3,)),
        ],
        compiler_params=limit(16),
        name="spectra",
    )(*(in_hbm(value) for value in (channel_to_slot[None, :], window, input_flags, voltages)))
    placed = lax.all_to_all(slotted, ("chan", "x"), split_axis=0, concat_axis=0, tiled=True)
    packed = pl.pallas_call(
        pack_kernel,
        out_shape=jax.ShapeDtypeStruct((GROUPS, BUNDLE, LANES), bf16),
        in_specs=[vmem],
        out_specs=vmem,
        compiler_params=limit(8),
        name="pack",
    )(placed)
    own = lax.all_to_all(packed, ("zh", "zl"), split_axis=0, concat_axis=0, tiled=True)
    other = lax.ppermute(own, "inp", [(0, 1), (1, 0)])
    depth = GROUPS * 64
    left, prod = pl.pallas_call(
        own_kernel,
        out_shape=(jax.ShapeDtypeStruct((512, depth), bf16), jax.ShapeDtypeStruct((512, 4 * LANES), f32)),
        in_specs=[vmem],
        out_specs=(vmem, vmem),
        compiler_params=limit(8),
        cost_estimate=pl.CostEstimate(flops=2 * 512 * 512 * 512, bytes_accessed=3 * 2**20, transcendentals=0),
        name="own",
    )(own)
    rows = pl.pallas_call(
        other_kernel,
        out_shape=jax.ShapeDtypeStruct((8, PARCEL, LANES), bf16),
        in_specs=[vmem, vmem, vmem],
        out_specs=vmem,
        scratch_shapes=[VMEM((512, 10 * LANES), f32)],
        compiler_params=limit(12),
        name="other",
    )(left, prod, other)
    parts = lax.all_to_all(rows, ("zl", "x"), split_axis=0, concat_axis=0, tiled=True)
    tiles = pl.pallas_call(
        tiles_kernel,
        out_shape=jax.ShapeDtypeStruct((OWNER_SLOTS, 64, KT * BLK), f32),
        in_specs=[vmem],
        out_specs=hbm,
        scratch_shapes=[VMEM((OWNER_SLOTS, 64, KT * BLK), f32), pltpu.SemaphoreType.DMA((OWNER_SLOTS,))],
        compiler_params=limit(8),
        name="tiles",
    )(parts)
    return tiles.reshape(OWNER_SLOTS, 1, 2, BLK, KT * BLK)


def solution(mesh):
    parts = Mesh(mesh.devices.reshape(2, 8, 4, 2, 4), ("inp", "chan", "zh", "zl", "x"))
    return jax.shard_map(
        on_device,
        mesh=parts,
        in_specs=(P(("inp", "chan"), ("zh", "zl", "x")), P(("inp", "chan"), None), P()),
        out_specs=P("chan", ("inp", "zh", "zl", "x"), None, None, None),
        check_vma=False,
    )
```

```python
import math

import jax
import jax.numpy as jnp
import numpy as np
from jax import lax
from jax.experimental import pallas as pl
from jax.experimental.pallas import tpu as pltpu
from jax.sharding import Mesh, PartitionSpec as P

FRAME_SAMPLES = 2048
NCHAN = 1024
TAPS = 4
SLOTS = 32
FRAMES = 8
IN_DEV = 128
LANES = 128
BLK = 32
KT = 34
OWNER_SLOTS = 4
GROUPS = 8
HELD = 5
MESSAGE = 24
SLICE = 64
BUNDLE = HELD * SLICE + 32
CUT = 18 * BLK
PARCEL = 4 * 64 + 32
CARRY = TAPS - 1
SPECTRUM_SCALE = 2.0**-7
NT = (((1,), (1,)), ((), ()))
VMEM = pltpu.VMEM


def window_table():
    sample = np.arange(TAPS * FRAME_SAMPLES, dtype=np.float64)
    middle = (sample + 0.5 - 0.5 * TAPS * FRAME_SAMPLES) / FRAME_SAMPLES
    hanning = 0.5 - 0.5 * np.cos(2.0 * math.pi * (sample + 0.5) / (TAPS * FRAME_SAMPLES))
    return (np.sinc(middle) * hanning).reshape(TAPS, FRAME_SAMPLES).astype(np.float32)


def spectra_kernel(
    slots_hbm, window_hbm, flags_hbm, volts_hbm, out_ref, slots, window, volts, table, flags, rows, sems
):
    small = []
    for index, (source, target) in enumerate(((slots_hbm, slots), (window_hbm, window), (flags_hbm, flags))):
        small.append(pltpu.make_async_copy(source, target, sems.at[FRAMES + index]))
        small[-1].start()
    copies = []
    for frame in range(FRAMES):
        copy = pltpu.make_async_copy(
            volts_hbm.at[:, pl.ds(frame * FRAME_SAMPLES, FRAME_SAMPLES)],
            volts.at[frame // 2, pl.ds(frame % 2 * IN_DEV, IN_DEV), :],
            sems.at[frame],
        )
        copy.start()
        copies.append(copy)

    small[0].wait()
    chosen = lax.broadcasted_iota(jnp.int32, (SLOTS, NCHAN), 0) == slots[...]
    channel = jnp.sum(
        jnp.where(chosen, lax.broadcasted_iota(jnp.int32, (SLOTS, NCHAN), 1), 0).astype(jnp.float32), 1, keepdims=True
    ).astype(jnp.int32)
    lane = lax.broadcasted_iota(jnp.int32, (SLOTS, LANES), 1)
    turn = 2.0 * math.pi / FRAME_SAMPLES
    fine = ((channel * lane) & (FRAME_SAMPLES - 1)).astype(jnp.float32) * turn
    coarse = ((channel * (lane * LANES)) & (FRAME_SAMPLES - 1)).astype(jnp.float32) * turn
    fine_cos, fine_sin = jnp.cos(fine), jnp.sin(fine)
    coarse_cos, coarse_sin = jnp.cos(coarse), jnp.sin(coarse)
    small[1].wait()
    for piece in range(FRAME_SAMPLES // LANES):
        at = pl.ds(piece * LANES, LANES)
        ccos, csin = coarse_cos[:, piece : piece + 1], coarse_sin[:, piece : piece + 1]
        cosine = (ccos * fine_cos - csin * fine_sin).astype(jnp.bfloat16).astype(jnp.float32)
        sine = (-(csin * fine_cos + ccos * fine_sin)).astype(jnp.bfloat16).astype(jnp.float32)
        for tap in range(TAPS):
            weight = window[tap : tap + 1, at]
            table[pl.ds(tap * 64, 32), at] = (cosine * weight).astype(jnp.bfloat16)
            table[pl.ds(tap * 64 + 32, 32), at] = (sine * weight).astype(jnp.bfloat16)

    small[2].wait()
    kept = lax.dot_general(
        chosen.astype(jnp.float32).astype(jnp.bfloat16),
        flags[...].astype(jnp.float32).astype(jnp.bfloat16),
        NT,
        preferred_element_type=jnp.float32,
    )

    sums = {}
    for pair in range(FRAMES // 2):
        if pair % 2 == 0:
            for copy in copies[2 * pair : 2 * pair + 4]:
                copy.wait()
        terms = lax.dot_general(table[...], volts[pair], NT, preferred_element_type=jnp.float32)
        for half in range(2):
            for tap in range(TAPS):
                frame = 2 * pair + half + TAPS - 1 - tap
                term = terms[tap * 64 : tap * 64 + 64, half * IN_DEV : (half + 1) * IN_DEV]
                sums[frame] = term if frame not in sums else sums[frame] + term
        for frame in [f for f in sums if f < 2 * pair + 2]:
            done = sums.pop(frame)
            rows[pl.ds(frame, SLOTS, stride=MESSAGE), :] = done[:32] * kept
            rows[pl.ds(FRAMES + frame, SLOTS, stride=MESSAGE), :] = done[32:] * kept
    empty = jnp.zeros((SLOTS, LANES), jnp.float32)
    for frame in range(CARRY + 1):
        real, imag = (sums[FRAMES + frame][:32] * kept, sums[FRAMES + frame][32:] * kept) if frame < CARRY else (empty, empty)
        rows[pl.ds(2 * FRAMES + frame, SLOTS, stride=MESSAGE), :] = real
        rows[pl.ds(2 * FRAMES + 4 + frame, SLOTS, stride=MESSAGE), :] = imag
    out_ref[...] = rows[pl.ds(0, SLOTS * MESSAGE), :].reshape(SLOTS, MESSAGE, LANES).astype(jnp.bfloat16)


def with_carry(real, imag, carried):
    axis = real.ndim - 2
    early = lax.broadcasted_iota(jnp.int32, real.shape, axis) < CARRY
    return real + jnp.where(early, carried, 0.0), imag + jnp.where(early, pltpu.roll(carried, 4, axis), 0.0)


def pack_kernel(in_ref, out_ref):
    slices, sums = [], []
    for group in range(GROUPS):
        pieces, carried = [], None
        for source in range(4):
            message = in_ref[4 * group + source].astype(jnp.float32)
            real, imag = message[:8], message[8:16]
            if source:
                real, imag = with_carry(real, imag, carried)
            pieces += [real, imag]
            carried = message[16:]
        slices.append(jnp.concatenate(pieces, 0).astype(jnp.bfloat16))
        sums.append(carried)
    unused = lax.broadcasted_iota(jnp.int32, (8, LANES), 0) % 4 == CARRY
    for target in range(GROUPS):
        parity = target % 2
        extra = target + 1 - 2 * parity
        taken = [parity + 2 * i for i in range(4)]
        for place, group in enumerate(taken + [extra]):
            out_ref[target, pl.ds(place * SLICE, SLICE), :] = slices[group]
        last = [
            jnp.where(unused, pltpu.roll(sums[extra], CARRY - i, 0), sums[group]) if i < CARRY else sums[group]
            for i, group in enumerate(taken)
        ]
        out_ref[target, pl.ds(HELD * SLICE, 32), :] = jnp.concatenate(last, 0).astype(jnp.bfloat16)


def joined(ref, place):
    start = place * SLICE if isinstance(place, int) else pl.multiple_of(place * SLICE, SLICE)
    block = ref[:, pl.ds(start, SLICE), :]
    early = block[:, :16].astype(jnp.float32)
    sums = ref[: GROUPS - 1, pl.ds(HELD * SLICE, 32), :].astype(jnp.float32)
    sums = [sums[:, 8 * i : 8 * i + 8] for i in range(4)]
    if not isinstance(place, int):
        carried = sum(jnp.where(place == i, sums[i], 0.0) for i in range(4))
    elif place < 4:
        carried = sums[place]
    else:
        row = lax.broadcasted_iota(jnp.int32, sums[0].shape, 1) % 4
        carried = sum(jnp.where(row == i, pltpu.roll(sums[i], 5 + i, 1), 0.0) for i in range(CARRY))
    carried = jnp.concatenate([jnp.zeros((1, 8, LANES), jnp.float32), carried], 0)
    early = jnp.concatenate(with_carry(early[:, :8], early[:, 8:], carried), 1).astype(jnp.bfloat16)
    return jnp.concatenate([early, block[:, 16:]], 1).reshape(GROUPS * SLICE, LANES)


def columns(ref, pair):
    return jnp.concatenate([joined(ref, 2 * pair + i) for i in range(2)], 1)


def own_kernel(own_ref, left_ref, prod_ref):
    same = lax.broadcasted_iota(jnp.int32, (LANES, LANES), 0) == lax.broadcasted_iota(jnp.int32, (LANES, LANES), 1)
    same = same.astype(jnp.float32).astype(jnp.bfloat16)
    depth = GROUPS * 64
    for kind, place in enumerate((lax.axis_index("zh"), HELD - 1)):
        straight = joined(own_ref, place)
        split = straight.astype(jnp.float32).reshape(depth // 16, 16, LANES)
        turned = jnp.concatenate([split[:, 8:], -split[:, :8]], 1).reshape(depth, LANES).astype(jnp.bfloat16)
        for half, value in enumerate((straight, turned)):
            left_ref[pl.ds(kind * 256 + half * LANES, LANES), :] = lax.dot_general(
                same, value, NT, preferred_element_type=jnp.float32
            ).astype(jnp.bfloat16)
    for pair in range(2):
        prod_ref[:, pl.ds(pair * 256, 256)] = jnp.dot(
            left_ref[...], columns(own_ref, pair), preferred_element_type=jnp.float32
        )


def other_kernel(left_ref, prod_ref, other_ref, out_ref, ring):
    zh, zl = lax.axis_index("zh"), lax.axis_index("zl")
    ring[:, pl.ds(LANES, 4 * LANES)] = prod_ref[...]
    ring[:, pl.ds(9 * LANES, LANES)] = prod_ref[:, :LANES]
    for pair in range(2):
        value = jnp.dot(left_ref[...], columns(other_ref, pair), preferred_element_type=jnp.float32)
        ring[:, pl.ds((5 + 2 * pair) * LANES, 2 * LANES)] = value
        if pair == 1:
            ring[:, pl.ds(0, LANES)] = value[:, LANES:]
    lane = lax.broadcasted_iota(jnp.int32, (BLK, LANES), 1)
    for kind in range(2):
        target = (zl if kind == 0 else 1 - zl) * 4
        for x in range(4):
            first = zh if kind == 0 else zh - zl + (1 if x else 0)
            start = pl.multiple_of((first + 1) * LANES, LANES)
            skipped = (x + 3) % 4 * BLK
            leads = (kind == 0) == (x > 0)
            lasts = []
            for half in range(2):
                value = ring[pl.ds(kind * 256 + half * LANES + x * BLK, BLK), pl.ds(start, 5 * LANES)]
                groups = [value[:, i * LANES : (i + 1) * LANES] for i in range(5)]
                if skipped:
                    groups = [pltpu.roll(group, LANES - skipped, 1) for group in groups]
                lasts.append(groups[4][:, : LANES // 2])
                if leads and skipped:
                    groups[0] = jnp.where(lane < LANES - skipped, groups[0], groups[4])
                for tile in range(4):
                    out_ref[target + x, pl.ds(tile * 64 + half * BLK, BLK), :] = groups[tile].astype(jnp.bfloat16)
            out_ref[target + x, pl.ds(256, BLK), :] = jnp.concatenate(lasts, 1).astype(jnp.bfloat16)


def tiles_kernel(in_ref, out_hbm, tiles, sems):
    zl, x = lax.axis_index("zl"), lax.axis_index("x")
    leading = lax.rem(zl + jnp.where(x == 0, 1, 0), 2)
    first = lax.broadcasted_iota(jnp.int32, (64, LANES), 1) < LANES - lax.rem(x + 3, 4) * BLK
    copies = []
    for slot in range(OWNER_SLOTS):
        sides = []
        for parity in (leading, 1 - leading):
            wide = in_ref[parity * 4 + slot].astype(jnp.float32)
            last = wide[256:]
            sides.append([wide[64 * i : 64 * i + 64] for i in range(4)] + [
                jnp.concatenate([last, pltpu.roll(last, LANES // 2, 1)], 0)
            ])
        even, odd = sides
        for i in range(4):
            tiles[slot, :, pl.ds(2 * i * LANES, LANES)] = jnp.where(first, even[i], odd[i])
            tiles[slot, :, pl.ds((2 * i + 1) * LANES, LANES)] = jnp.where(first, odd[i], even[(i + 1) % 4])
        tiles[slot, :, pl.ds(8 * LANES, LANES // 2)] = jnp.where(first, even[4], odd[4])[:, : LANES // 2]
        copies.append(pltpu.make_async_copy(tiles.at[slot], out_hbm.at[slot], sems.at[slot]))
        copies[-1].start()
    for copy in copies:
        copy.wait()


def on_device(voltages, input_flags, channel_to_slot):
    hbm = pl.BlockSpec(memory_space=pltpu.HBM)
    vmem = pl.BlockSpec(memory_space=VMEM)
    f32, bf16 = jnp.float32, jnp.bfloat16
    limit = lambda mib: pltpu.CompilerParams(vmem_limit_bytes=mib * 2**20)
    in_hbm = lambda value: pltpu.with_memory_space_constraint(value, pltpu.HBM)
    window = jnp.asarray(window_table() * np.float32(SPECTRUM_SCALE))
    slotted = pl.pallas_call(
        spectra_kernel,
        out_shape=VMEM((SLOTS, MESSAGE, LANES), bf16),
        in_specs=[hbm, hbm, hbm, hbm],
        out_specs=vmem,
        scratch_shapes=[
            VMEM((1, NCHAN), jnp.int32),
            VMEM((TAPS, FRAME_SAMPLES), f32),
            VMEM((FRAMES // 2, 2 * IN_DEV, FRAME_SAMPLES), bf16),
            VMEM((TAPS * 64, FRAME_SAMPLES), bf16),
            VMEM((IN_DEV, NCHAN), jnp.int32),
            VMEM(((SLOTS + 1) * MESSAGE, LANES), f32),
            pltpu.SemaphoreType.DMA((FRAMES + 3,)),
        ],
        compiler_params=limit(16),
        name="spectra",
    )(*(in_hbm(value) for value in (channel_to_slot[None, :], window, input_flags, voltages)))
    placed = lax.all_to_all(slotted, ("chan", "x"), split_axis=0, concat_axis=0, tiled=True)
    packed = pl.pallas_call(
        pack_kernel,
        out_shape=jax.ShapeDtypeStruct((GROUPS, BUNDLE, LANES), bf16),
        in_specs=[vmem],
        out_specs=vmem,
        compiler_params=limit(8),
        name="pack",
    )(placed)
    own = lax.all_to_all(packed, ("zh", "zl"), split_axis=0, concat_axis=0, tiled=True)
    other = lax.ppermute(own, "inp", [(0, 1), (1, 0)])
    depth = GROUPS * 64
    left, prod = pl.pallas_call(
        own_kernel,
        out_shape=(jax.ShapeDtypeStruct((512, depth), bf16), jax.ShapeDtypeStruct((512, 4 * LANES), f32)),
        in_specs=[vmem],
        out_specs=(vmem, vmem),
        compiler_params=limit(8),
        cost_estimate=pl.CostEstimate(flops=2 * 512 * 512 * 512, bytes_accessed=3 * 2**20, transcendentals=0),
        name="own",
    )(own)
    rows = pl.pallas_call(
        other_kernel,
        out_shape=jax.ShapeDtypeStruct((8, PARCEL, LANES), bf16),
        in_specs=[vmem, vmem, vmem],
        out_specs=vmem,
        scratch_shapes=[VMEM((512, 10 * LANES), f32)],
        compiler_params=limit(12),
        name="other",
    )(left, prod, other)
    parts = lax.all_to_all(rows, ("zl", "x"), split_axis=0, concat_axis=0, tiled=True)
    tiles = pl.pallas_call(
        tiles_kernel,
        out_shape=jax.ShapeDtypeStruct((OWNER_SLOTS, 64, KT * BLK), f32),
        in_specs=[vmem],
        out_specs=hbm,
        scratch_shapes=[VMEM((OWNER_SLOTS, 64, KT * BLK), f32), pltpu.SemaphoreType.DMA((OWNER_SLOTS,))],
        compiler_params=limit(8),
        name="tiles",
    )(parts)
    return tiles.reshape(OWNER_SLOTS, 1, 2, BLK, KT * BLK)


def solution(mesh):
    parts = Mesh(mesh.devices.reshape(2, 8, 4, 2, 4), ("inp", "chan", "zh", "zl", "x"))
    return jax.shard_map(
        on_device,
        mesh=parts,
        in_specs=(P(("inp", "chan"), ("zh", "zl", "x")), P(("inp", "chan"), None), P()),
        out_specs=P("chan", ("inp", "zh", "zl", "x"), None, None, None),
        check_vma=False,
    )
```

```python
import math

import jax
import jax.numpy as jnp
import numpy as np
from jax import lax
from jax.experimental import pallas as pl
from jax.experimental.pallas import tpu as pltpu
from jax.sharding import Mesh, PartitionSpec as P

FRAME_SAMPLES = 2048
NCHAN = 1024
TAPS = 4
SLOTS = 32
FRAMES = 8
IN_DEV = 128
LANES = 128
BLK = 32
KT = 34
OWNER_SLOTS = 4
GROUPS = 8
HELD = 5
MESSAGE = 24
SLICE = 64
SUMS = 4 * SLICE
EXTRA = SUMS + 32
BUNDLE = EXTRA + SLICE
CUT = 18 * BLK
PARCEL = 4 * 64 + 32
CARRY = TAPS - 1
SPECTRUM_SCALE = 2.0**-7
NT = (((1,), (1,)), ((), ()))
VMEM = pltpu.VMEM


def window_table():
    sample = np.arange(TAPS * FRAME_SAMPLES, dtype=np.float64)
    middle = (sample + 0.5 - 0.5 * TAPS * FRAME_SAMPLES) / FRAME_SAMPLES
    hanning = 0.5 - 0.5 * np.cos(2.0 * math.pi * (sample + 0.5) / (TAPS * FRAME_SAMPLES))
    return (np.sinc(middle) * hanning).reshape(TAPS, FRAME_SAMPLES).astype(np.float32)


def spectra_kernel(
    slots_hbm, window_hbm, flags_hbm, volts_hbm, out_ref, slots, window, volts, table, flags, rows, sems
):
    small = []
    for index, (source, target) in enumerate(((slots_hbm, slots), (window_hbm, window), (flags_hbm, flags))):
        small.append(pltpu.make_async_copy(source, target, sems.at[FRAMES + index]))
        small[-1].start()
    copies = []
    for frame in range(FRAMES):
        copy = pltpu.make_async_copy(
            volts_hbm.at[:, pl.ds(frame * FRAME_SAMPLES, FRAME_SAMPLES)],
            volts.at[frame // 2, pl.ds(frame % 2 * IN_DEV, IN_DEV), :],
            sems.at[frame],
        )
        copy.start()
        copies.append(copy)

    small[0].wait()
    chosen = lax.broadcasted_iota(jnp.int32, (SLOTS, NCHAN), 0) == slots[...]
    channel = jnp.sum(
        jnp.where(chosen, lax.broadcasted_iota(jnp.int32, (SLOTS, NCHAN), 1), 0).astype(jnp.float32), 1, keepdims=True
    ).astype(jnp.int32)
    lane = lax.broadcasted_iota(jnp.int32, (SLOTS, LANES), 1)
    turn = 2.0 * math.pi / FRAME_SAMPLES
    fine = ((channel * lane) & (FRAME_SAMPLES - 1)).astype(jnp.float32) * turn
    coarse = ((channel * (lane * LANES)) & (FRAME_SAMPLES - 1)).astype(jnp.float32) * turn
    fine_cos, fine_sin = jnp.cos(fine), jnp.sin(fine)
    coarse_cos, coarse_sin = jnp.cos(coarse), jnp.sin(coarse)
    small[1].wait()
    for piece in range(FRAME_SAMPLES // LANES):
        at = pl.ds(piece * LANES, LANES)
        ccos, csin = coarse_cos[:, piece : piece + 1], coarse_sin[:, piece : piece + 1]
        cosine = (ccos * fine_cos - csin * fine_sin).astype(jnp.bfloat16).astype(jnp.float32)
        sine = (-(csin * fine_cos + ccos * fine_sin)).astype(jnp.bfloat16).astype(jnp.float32)
        for tap in range(TAPS):
            weight = window[tap : tap + 1, at]
            table[pl.ds(tap * 64, 32), at] = (cosine * weight).astype(jnp.bfloat16)
            table[pl.ds(tap * 64 + 32, 32), at] = (sine * weight).astype(jnp.bfloat16)

    small[2].wait()
    kept = lax.dot_general(
        chosen.astype(jnp.float32).astype(jnp.bfloat16),
        flags[...].astype(jnp.float32).astype(jnp.bfloat16),
        NT,
        preferred_element_type=jnp.float32,
    )

    sums = {}
    for pair in range(FRAMES // 2):
        if pair % 2 == 0:
            for copy in copies[2 * pair : 2 * pair + 4]:
                copy.wait()
        terms = lax.dot_general(table[...], volts[pair], NT, preferred_element_type=jnp.float32)
        for half in range(2):
            for tap in range(TAPS):
                frame = 2 * pair + half + TAPS - 1 - tap
                term = terms[tap * 64 : tap * 64 + 64, half * IN_DEV : (half + 1) * IN_DEV]
                sums[frame] = term if frame not in sums else sums[frame] + term
        for frame in [f for f in sums if f < 2 * pair + 2]:
            done = sums.pop(frame)
            rows[pl.ds(frame, SLOTS, stride=MESSAGE), :] = done[:32] * kept
            rows[pl.ds(FRAMES + frame, SLOTS, stride=MESSAGE), :] = done[32:] * kept
    empty = jnp.zeros((SLOTS, LANES), jnp.float32)
    for frame in range(CARRY + 1):
        real, imag = (sums[FRAMES + frame][:32] * kept, sums[FRAMES + frame][32:] * kept) if frame < CARRY else (empty, empty)
        rows[pl.ds(2 * FRAMES + frame, SLOTS, stride=MESSAGE), :] = real
        rows[pl.ds(2 * FRAMES + 4 + frame, SLOTS, stride=MESSAGE), :] = imag
    out_ref[...] = rows[pl.ds(0, SLOTS * MESSAGE), :].reshape(SLOTS, MESSAGE, LANES).astype(jnp.bfloat16)


def with_carry(real, imag, carried):
    axis = real.ndim - 2
    early = lax.broadcasted_iota(jnp.int32, real.shape, axis) < CARRY
    return real + jnp.where(early, carried, 0.0), imag + jnp.where(early, pltpu.roll(carried, 4, axis), 0.0)


def pack_kernel(in_ref, out_ref):
    slices, sums = [], []
    for group in range(GROUPS):
        pieces, carried = [], None
        for source in range(4):
            message = in_ref[4 * group + source].astype(jnp.float32)
            real, imag = message[:8], message[8:16]
            if source:
                real, imag = with_carry(real, imag, carried)
            pieces += [real, imag]
            carried = message[16:]
        slices.append(jnp.concatenate(pieces, 0).astype(jnp.bfloat16))
        sums.append(carried)
    unused = lax.broadcasted_iota(jnp.int32, (8, LANES), 0) % 4 == CARRY
    for target in range(GROUPS):
        parity = target % 2
        extra = target + 1 - 2 * parity
        taken = [parity + 2 * i for i in range(4)]
        for place, group in enumerate(taken + [extra]):
            out_ref[target, pl.ds(place * SLICE if place < 4 else EXTRA, SLICE), :] = slices[group]
        last = [
            jnp.where(unused, pltpu.roll(sums[extra], CARRY - i, 0), sums[group]) if i < CARRY else sums[group]
            for i, group in enumerate(taken)
        ]
        out_ref[target, pl.ds(SUMS, 32), :] = jnp.concatenate(last, 0).astype(jnp.bfloat16)


def joined(ref, place):
    if isinstance(place, int):
        start = place * SLICE if place < 4 else EXTRA
    else:
        start = pl.multiple_of(place * SLICE, SLICE)
    block = ref[:, pl.ds(start, SLICE), :]
    early = block[:, :16].astype(jnp.float32)
    sums = ref[: GROUPS - 1, pl.ds(SUMS, 32), :].astype(jnp.float32)
    sums = [sums[:, 8 * i : 8 * i + 8] for i in range(4)]
    if not isinstance(place, int):
        carried = sum(jnp.where(place == i, sums[i], 0.0) for i in range(4))
    elif place < 4:
        carried = sums[place]
    else:
        row = lax.broadcasted_iota(jnp.int32, sums[0].shape, 1) % 4
        carried = sum(jnp.where(row == i, pltpu.roll(sums[i], 5 + i, 1), 0.0) for i in range(CARRY))
    carried = jnp.concatenate([jnp.zeros((1, 8, LANES), jnp.float32), carried], 0)
    early = jnp.concatenate(with_carry(early[:, :8], early[:, 8:], carried), 1).astype(jnp.bfloat16)
    return jnp.concatenate([early, block[:, 16:]], 1).reshape(GROUPS * SLICE, LANES)


def columns(ref, pair):
    return jnp.concatenate([joined(ref, 2 * pair + i) for i in range(2)], 1)


def own_kernel(own_ref, left_ref, prod_ref):
    same = lax.broadcasted_iota(jnp.int32, (LANES, LANES), 0) == lax.broadcasted_iota(jnp.int32, (LANES, LANES), 1)
    same = same.astype(jnp.float32).astype(jnp.bfloat16)
    depth = GROUPS * 64
    for kind, place in enumerate((lax.axis_index("zh"), HELD - 1)):
        straight = joined(own_ref, place)
        split = straight.astype(jnp.float32).reshape(depth // 16, 16, LANES)
        turned = jnp.concatenate([split[:, 8:], -split[:, :8]], 1).reshape(depth, LANES).astype(jnp.bfloat16)
        for half, value in enumerate((straight, turned)):
            left_ref[pl.ds(kind * 256 + half * LANES, LANES), :] = lax.dot_general(
                same, value, NT, preferred_element_type=jnp.float32
            ).astype(jnp.bfloat16)
    for pair in range(2):
        prod_ref[:, pl.ds(pair * 256, 256)] = jnp.dot(
            left_ref[...], columns(own_ref, pair), preferred_element_type=jnp.float32
        )


def other_kernel(left_ref, prod_ref, other_ref, out_ref, ring):
    zh, zl = lax.axis_index("zh"), lax.axis_index("zl")
    ring[:, pl.ds(LANES, 4 * LANES)] = prod_ref[...]
    ring[:, pl.ds(9 * LANES, LANES)] = prod_ref[:, :LANES]
    for pair in range(2):
        value = jnp.dot(left_ref[...], columns(other_ref, pair), preferred_element_type=jnp.float32)
        ring[:, pl.ds((5 + 2 * pair) * LANES, 2 * LANES)] = value
        if pair == 1:
            ring[:, pl.ds(0, LANES)] = value[:, LANES:]
    lane = lax.broadcasted_iota(jnp.int32, (BLK, LANES), 1)
    for kind in range(2):
        target = (zl if kind == 0 else 1 - zl) * 4
        for x in range(4):
            first = zh if kind == 0 else zh - zl + (1 if x else 0)
            start = pl.multiple_of((first + 1) * LANES, LANES)
            skipped = (x + 3) % 4 * BLK
            leads = (kind == 0) == (x > 0)
            lasts = []
            for half in range(2):
                value = ring[pl.ds(kind * 256 + half * LANES + x * BLK, BLK), pl.ds(start, 5 * LANES)]
                groups = [value[:, i * LANES : (i + 1) * LANES] for i in range(5)]
                if skipped:
                    groups = [pltpu.roll(group, LANES - skipped, 1) for group in groups]
                lasts.append(groups[4][:, : LANES // 2])
                if leads and skipped:
                    groups[0] = jnp.where(lane < LANES - skipped, groups[0], groups[4])
                for tile in range(4):
                    out_ref[target + x, pl.ds(tile * 64 + half * BLK, BLK), :] = groups[tile].astype(jnp.bfloat16)
            out_ref[target + x, pl.ds(256, BLK), :] = jnp.concatenate(lasts, 1).astype(jnp.bfloat16)


def tiles_kernel(in_ref, out_hbm, tiles, sems):
    zl, x = lax.axis_index("zl"), lax.axis_index("x")
    leading = lax.rem(zl + jnp.where(x == 0, 1, 0), 2)
    first = lax.broadcasted_iota(jnp.int32, (64, LANES), 1) < LANES - lax.rem(x + 3, 4) * BLK
    copies = []
    for slot in range(OWNER_SLOTS):
        sides = []
        for parity in (leading, 1 - leading):
            wide = in_ref[parity * 4 + slot].astype(jnp.float32)
            last = wide[256:]
            sides.append([wide[64 * i : 64 * i + 64] for i in range(4)] + [
                jnp.concatenate([last, pltpu.roll(last, LANES // 2, 1)], 0)
            ])
        even, odd = sides
        for i in range(4):
            tiles[slot, :, pl.ds(2 * i * LANES, LANES)] = jnp.where(first, even[i], odd[i])
            tiles[slot, :, pl.ds((2 * i + 1) * LANES, LANES)] = jnp.where(first, odd[i], even[(i + 1) % 4])
        tiles[slot, :, pl.ds(8 * LANES, LANES // 2)] = jnp.where(first, even[4], odd[4])[:, : LANES // 2]
        copies.append(pltpu.make_async_copy(tiles.at[slot], out_hbm.at[slot], sems.at[slot]))
        copies[-1].start()
    for copy in copies:
        copy.wait()


def on_device(voltages, input_flags, channel_to_slot):
    hbm = pl.BlockSpec(memory_space=pltpu.HBM)
    vmem = pl.BlockSpec(memory_space=VMEM)
    f32, bf16 = jnp.float32, jnp.bfloat16
    limit = lambda mib: pltpu.CompilerParams(vmem_limit_bytes=mib * 2**20)
    in_hbm = lambda value: pltpu.with_memory_space_constraint(value, pltpu.HBM)
    window = jnp.asarray(window_table() * np.float32(SPECTRUM_SCALE))
    slotted = pl.pallas_call(
        spectra_kernel,
        out_shape=VMEM((SLOTS, MESSAGE, LANES), bf16),
        in_specs=[hbm, hbm, hbm, hbm],
        out_specs=vmem,
        scratch_shapes=[
            VMEM((1, NCHAN), jnp.int32),
            VMEM((TAPS, FRAME_SAMPLES), f32),
            VMEM((FRAMES // 2, 2 * IN_DEV, FRAME_SAMPLES), bf16),
            VMEM((TAPS * 64, FRAME_SAMPLES), bf16),
            VMEM((IN_DEV, NCHAN), jnp.int32),
            VMEM(((SLOTS + 1) * MESSAGE, LANES), f32),
            pltpu.SemaphoreType.DMA((FRAMES + 3,)),
        ],
        compiler_params=limit(16),
        name="spectra",
    )(*(in_hbm(value) for value in (channel_to_slot[None, :], window, input_flags, voltages)))
    placed = lax.all_to_all(slotted, ("chan", "x"), split_axis=0, concat_axis=0, tiled=True)
    packed = pl.pallas_call(
        pack_kernel,
        out_shape=jax.ShapeDtypeStruct((GROUPS, BUNDLE, LANES), bf16),
        in_specs=[vmem],
        out_specs=vmem,
        compiler_params=limit(8),
        name="pack",
    )(placed)
    own = lax.all_to_all(packed, ("zh", "zl"), split_axis=0, concat_axis=0, tiled=True)
    other = lax.ppermute(own[:, :EXTRA], "inp", [(0, 1), (1, 0)])
    depth = GROUPS * 64
    left, prod = pl.pallas_call(
        own_kernel,
        out_shape=(jax.ShapeDtypeStruct((512, depth), bf16), jax.ShapeDtypeStruct((512, 4 * LANES), f32)),
        in_specs=[vmem],
        out_specs=(vmem, vmem),
        compiler_params=limit(8),
        cost_estimate=pl.CostEstimate(flops=2 * 512 * 512 * 512, bytes_accessed=3 * 2**20, transcendentals=0),
        name="own",
    )(own)
    rows = pl.pallas_call(
        other_kernel,
        out_shape=jax.ShapeDtypeStruct((8, PARCEL, LANES), bf16),
        in_specs=[vmem, vmem, vmem],
        out_specs=vmem,
        scratch_shapes=[VMEM((512, 10 * LANES), f32)],
        compiler_params=limit(12),
        name="other",
    )(left, prod, other)
    parts = lax.all_to_all(rows, ("zl", "x"), split_axis=0, concat_axis=0, tiled=True)
    tiles = pl.pallas_call(
        tiles_kernel,
        out_shape=jax.ShapeDtypeStruct((OWNER_SLOTS, 64, KT * BLK), f32),
        in_specs=[vmem],
        out_specs=hbm,
        scratch_shapes=[VMEM((OWNER_SLOTS, 64, KT * BLK), f32), pltpu.SemaphoreType.DMA((OWNER_SLOTS,))],
        compiler_params=limit(8),
        name="tiles",
    )(parts)
    return tiles.reshape(OWNER_SLOTS, 1, 2, BLK, KT * BLK)


def solution(mesh):
    parts = Mesh(mesh.devices.reshape(2, 8, 4, 2, 4), ("inp", "chan", "zh", "zl", "x"))
    return jax.shard_map(
        on_device,
        mesh=parts,
        in_specs=(P(("inp", "chan"), ("zh", "zl", "x")), P(("inp", "chan"), None), P()),
        out_specs=P("chan", ("inp", "zh", "zl", "x"), None, None, None),
        check_vma=False,
    )
```

```python
import math

import jax
import jax.numpy as jnp
import numpy as np
from jax import lax
from jax.experimental import pallas as pl
from jax.experimental.pallas import tpu as pltpu
from jax.sharding import Mesh, PartitionSpec as P

FRAME_SAMPLES = 2048
NCHAN = 1024
TAPS = 4
SLOTS = 32
FRAMES = 8
IN_DEV = 128
LANES = 128
BLK = 32
KT = 34
OWNER_SLOTS = 4
GROUPS = 8
HELD = 5
MESSAGE = 24
SLICE = 64
SUMS = 4 * SLICE
EXTRA = SUMS + 32
BUNDLE = EXTRA + SLICE
CUT = 18 * BLK
PARCEL = 4 * 64 + 32
CARRY = TAPS - 1
SPECTRUM_SCALE = 2.0**-7
NT = (((1,), (1,)), ((), ()))
VMEM = pltpu.VMEM


def window_table():
    sample = np.arange(TAPS * FRAME_SAMPLES, dtype=np.float64)
    middle = (sample + 0.5 - 0.5 * TAPS * FRAME_SAMPLES) / FRAME_SAMPLES
    hanning = 0.5 - 0.5 * np.cos(2.0 * math.pi * (sample + 0.5) / (TAPS * FRAME_SAMPLES))
    return (np.sinc(middle) * hanning).reshape(TAPS, FRAME_SAMPLES).astype(np.float32)


def spectra_kernel(
    slots_hbm, window_hbm, flags_hbm, volts_hbm, out_ref, slots, window, volts, table, flags, rows, sems
):
    small = []
    for index, (source, target) in enumerate(((slots_hbm, slots), (window_hbm, window), (flags_hbm, flags))):
        small.append(pltpu.make_async_copy(source, target, sems.at[FRAMES + index]))
        small[-1].start()
    copies = []
    for frame in range(FRAMES):
        copy = pltpu.make_async_copy(
            volts_hbm.at[:, pl.ds(frame * FRAME_SAMPLES, FRAME_SAMPLES)],
            volts.at[frame // 2, pl.ds(frame % 2 * IN_DEV, IN_DEV), :],
            sems.at[frame],
        )
        copy.start()
        copies.append(copy)

    small[0].wait()
    chosen = lax.broadcasted_iota(jnp.int32, (SLOTS, NCHAN), 0) == slots[...]
    channel = jnp.sum(
        jnp.where(chosen, lax.broadcasted_iota(jnp.int32, (SLOTS, NCHAN), 1), 0).astype(jnp.float32), 1, keepdims=True
    ).astype(jnp.int32)
    lane = lax.broadcasted_iota(jnp.int32, (SLOTS, LANES), 1)
    turn = 2.0 * math.pi / FRAME_SAMPLES
    fine = ((channel * lane) & (FRAME_SAMPLES - 1)).astype(jnp.float32) * turn
    coarse = ((channel * (lane * LANES)) & (FRAME_SAMPLES - 1)).astype(jnp.float32) * turn
    fine_cos, fine_sin = jnp.cos(fine), jnp.sin(fine)
    coarse_cos, coarse_sin = jnp.cos(coarse), jnp.sin(coarse)
    small[1].wait()
    for piece in range(FRAME_SAMPLES // LANES):
        at = pl.ds(piece * LANES, LANES)
        ccos, csin = coarse_cos[:, piece : piece + 1], coarse_sin[:, piece : piece + 1]
        cosine = (ccos * fine_cos - csin * fine_sin).astype(jnp.bfloat16).astype(jnp.float32)
        sine = (-(csin * fine_cos + ccos * fine_sin)).astype(jnp.bfloat16).astype(jnp.float32)
        for tap in range(TAPS):
            weight = window[tap : tap + 1, at]
            table[pl.ds(tap * 64, 32), at] = (cosine * weight).astype(jnp.bfloat16)
            table[pl.ds(tap * 64 + 32, 32), at] = (sine * weight).astype(jnp.bfloat16)

    small[2].wait()
    kept = lax.dot_general(
        chosen.astype(jnp.float32).astype(jnp.bfloat16),
        flags[...].astype(jnp.float32).astype(jnp.bfloat16),
        NT,
        preferred_element_type=jnp.float32,
    )

    sums = {}
    for pair in range(FRAMES // 2):
        if pair % 2 == 0:
            for copy in copies[2 * pair : 2 * pair + 4]:
                copy.wait()
        terms = lax.dot_general(table[...], volts[pair], NT, preferred_element_type=jnp.float32)
        for half in range(2):
            for tap in range(TAPS):
                frame = 2 * pair + half + TAPS - 1 - tap
                term = terms[tap * 64 : tap * 64 + 64, half * IN_DEV : (half + 1) * IN_DEV]
                sums[frame] = term if frame not in sums else sums[frame] + term
        for frame in [f for f in sums if f < 2 * pair + 2]:
            done = sums.pop(frame)
            rows[pl.ds(frame, SLOTS, stride=MESSAGE), :] = done[:32] * kept
            rows[pl.ds(FRAMES + frame, SLOTS, stride=MESSAGE), :] = done[32:] * kept
    empty = jnp.zeros((SLOTS, LANES), jnp.float32)
    for frame in range(CARRY + 1):
        real, imag = (sums[FRAMES + frame][:32] * kept, sums[FRAMES + frame][32:] * kept) if frame < CARRY else (empty, empty)
        rows[pl.ds(2 * FRAMES + frame, SLOTS, stride=MESSAGE), :] = real
        rows[pl.ds(2 * FRAMES + 4 + frame, SLOTS, stride=MESSAGE), :] = imag
    out_ref[...] = rows[pl.ds(0, SLOTS * MESSAGE), :].reshape(SLOTS, MESSAGE, LANES).astype(jnp.bfloat16)


def with_carry(real, imag, carried):
    axis = real.ndim - 2
    early = lax.broadcasted_iota(jnp.int32, real.shape, axis) < CARRY
    return real + jnp.where(early, carried, 0.0), imag + jnp.where(early, pltpu.roll(carried, 4, axis), 0.0)


def pack_kernel(in_ref, out_ref):
    slices, sums = [], []
    for group in range(GROUPS):
        pieces, carried = [], None
        for source in range(4):
            message = in_ref[4 * group + source].astype(jnp.float32)
            real, imag = message[:8], message[8:16]
            if source:
                real, imag = with_carry(real, imag, carried)
            pieces += [real, imag]
            carried = message[16:]
        slices.append(jnp.concatenate(pieces, 0).astype(jnp.bfloat16))
        sums.append(carried)
    unused = lax.broadcasted_iota(jnp.int32, (8, LANES), 0) % 4 == CARRY
    for target in range(GROUPS):
        parity = target % 2
        extra = target + 1 - 2 * parity
        taken = [parity + 2 * i for i in range(4)]
        for place, group in enumerate(taken + [extra]):
            out_ref[target, pl.ds(place * SLICE if place < 4 else EXTRA, SLICE), :] = slices[group]
        last = [
            jnp.where(unused, pltpu.roll(sums[extra], CARRY - i, 0), sums[group]) if i < CARRY else sums[group]
            for i, group in enumerate(taken)
        ]
        out_ref[target, pl.ds(SUMS, 32), :] = jnp.concatenate(last, 0).astype(jnp.bfloat16)


def joined(ref, place):
    if isinstance(place, int):
        start = place * SLICE if place < 4 else EXTRA
    else:
        start = pl.multiple_of(place * SLICE, SLICE)
    block = ref[:, pl.ds(start, SLICE), :]
    early = block[:, :16].astype(jnp.float32)
    sums = ref[: GROUPS - 1, pl.ds(SUMS, 32), :].astype(jnp.float32)
    sums = [sums[:, 8 * i : 8 * i + 8] for i in range(4)]
    if not isinstance(place, int):
        carried = sum(jnp.where(place == i, sums[i], 0.0) for i in range(4))
    elif place < 4:
        carried = sums[place]
    else:
        row = lax.broadcasted_iota(jnp.int32, sums[0].shape, 1) % 4
        carried = sum(jnp.where(row == i, pltpu.roll(sums[i], 5 + i, 1), 0.0) for i in range(CARRY))
    carried = jnp.concatenate([jnp.zeros((1, 8, LANES), jnp.float32), carried], 0)
    early = jnp.concatenate(with_carry(early[:, :8], early[:, 8:], carried), 1).astype(jnp.bfloat16)
    return jnp.concatenate([early, block[:, 16:]], 1).reshape(GROUPS * SLICE, LANES)


def columns(ref, pair):
    return jnp.concatenate([joined(ref, 2 * pair + i) for i in range(2)], 1)


def put(ring, group, value):
    for block in range(16):
        skipped = (block + 3) % 4 * BLK
        for i in range(2):
            part = value[block * BLK : (block + 1) * BLK, i * LANES : (i + 1) * LANES]
            part = (pltpu.roll(part, LANES - skipped, 1) if skipped else part).astype(jnp.bfloat16)
            ring[pl.ds(block * BLK, BLK), pl.ds((group + 1 + i) * LANES, LANES)] = part
            if group + i in (0, 7):
                ring[pl.ds(block * BLK, BLK), pl.ds((9 if group + i == 0 else 0) * LANES, LANES)] = part


def own_kernel(own_ref, left_ref, ring_ref):
    same = lax.broadcasted_iota(jnp.int32, (LANES, LANES), 0) == lax.broadcasted_iota(jnp.int32, (LANES, LANES), 1)
    same = same.astype(jnp.float32).astype(jnp.bfloat16)
    depth = GROUPS * 64
    for kind, place in enumerate((lax.axis_index("zh"), HELD - 1)):
        straight = joined(own_ref, place)
        split = straight.astype(jnp.float32).reshape(depth // 16, 16, LANES)
        turned = jnp.concatenate([split[:, 8:], -split[:, :8]], 1).reshape(depth, LANES).astype(jnp.bfloat16)
        for half, value in enumerate((straight, turned)):
            left_ref[pl.ds(kind * 256 + half * LANES, LANES), :] = lax.dot_general(
                same, value, NT, preferred_element_type=jnp.float32
            ).astype(jnp.bfloat16)
    for pair in range(2):
        value = jnp.dot(left_ref[...], columns(own_ref, pair), preferred_element_type=jnp.float32)
        put(ring_ref, 2 * pair, value)


def other_kernel(left_ref, own_ring_ref, other_ref, out_ref, ring):
    del own_ring_ref
    zh, zl = lax.axis_index("zh"), lax.axis_index("zl")
    for pair in range(2):
        value = jnp.dot(left_ref[...], columns(other_ref, pair), preferred_element_type=jnp.float32)
        put(ring, 4 + 2 * pair, value)
    lane = lax.broadcasted_iota(jnp.int32, (BLK, LANES), 1)
    for kind in range(2):
        target = (zl if kind == 0 else 1 - zl) * 4
        for x in range(4):
            first = zh if kind == 0 else zh - zl + (1 if x else 0)
            start = pl.multiple_of((first + 1) * LANES, LANES)
            skipped = (x + 3) % 4 * BLK
            leads = (kind == 0) == (x > 0)
            lasts = []
            for half in range(2):
                row = kind * 256 + half * LANES + x * BLK
                groups = [ring[pl.ds(row, BLK), pl.ds(start + i * LANES, LANES)] for i in range(5)]
                fifth = groups[4].astype(jnp.float32)
                lasts.append(fifth[:, : LANES // 2])
                if leads and skipped:
                    head = jnp.where(lane < LANES - skipped, groups[0].astype(jnp.float32), fifth)
                    groups[0] = head.astype(jnp.bfloat16)
                for tile in range(4):
                    out_ref[target + x, pl.ds(tile * 64 + half * BLK, BLK), :] = groups[tile]
            out_ref[target + x, pl.ds(256, BLK), :] = jnp.concatenate(lasts, 1).astype(jnp.bfloat16)


def tiles_kernel(in_ref, out_hbm, tiles, sems):
    zl, x = lax.axis_index("zl"), lax.axis_index("x")
    leading = lax.rem(zl + jnp.where(x == 0, 1, 0), 2)
    first = lax.broadcasted_iota(jnp.int32, (64, LANES), 1) < LANES - lax.rem(x + 3, 4) * BLK
    copies = []
    for slot in range(OWNER_SLOTS):
        sides = []
        for parity in (leading, 1 - leading):
            wide = in_ref[parity * 4 + slot].astype(jnp.float32)
            last = wide[256:]
            sides.append([wide[64 * i : 64 * i + 64] for i in range(4)] + [
                jnp.concatenate([last, pltpu.roll(last, LANES // 2, 1)], 0)
            ])
        even, odd = sides
        for i in range(4):
            tiles[slot, :, pl.ds(2 * i * LANES, LANES)] = jnp.where(first, even[i], odd[i])
            tiles[slot, :, pl.ds((2 * i + 1) * LANES, LANES)] = jnp.where(first, odd[i], even[(i + 1) % 4])
        tiles[slot, :, pl.ds(8 * LANES, LANES // 2)] = jnp.where(first, even[4], odd[4])[:, : LANES // 2]
        copies.append(pltpu.make_async_copy(tiles.at[slot], out_hbm.at[slot], sems.at[slot]))
        copies[-1].start()
    for copy in copies:
        copy.wait()


def on_device(voltages, input_flags, channel_to_slot):
    hbm = pl.BlockSpec(memory_space=pltpu.HBM)
    vmem = pl.BlockSpec(memory_space=VMEM)
    f32, bf16 = jnp.float32, jnp.bfloat16
    limit = lambda mib: pltpu.CompilerParams(vmem_limit_bytes=mib * 2**20)
    in_hbm = lambda value: pltpu.with_memory_space_constraint(value, pltpu.HBM)
    window = jnp.asarray(window_table() * np.float32(SPECTRUM_SCALE))
    slotted = pl.pallas_call(
        spectra_kernel,
        out_shape=VMEM((SLOTS, MESSAGE, LANES), bf16),
        in_specs=[hbm, hbm, hbm, hbm],
        out_specs=vmem,
        scratch_shapes=[
            VMEM((1, NCHAN), jnp.int32),
            VMEM((TAPS, FRAME_SAMPLES), f32),
            VMEM((FRAMES // 2, 2 * IN_DEV, FRAME_SAMPLES), bf16),
            VMEM((TAPS * 64, FRAME_SAMPLES), bf16),
            VMEM((IN_DEV, NCHAN), jnp.int32),
            VMEM(((SLOTS + 1) * MESSAGE, LANES), f32),
            pltpu.SemaphoreType.DMA((FRAMES + 3,)),
        ],
        compiler_params=limit(16),
        name="spectra",
    )(*(in_hbm(value) for value in (channel_to_slot[None, :], window, input_flags, voltages)))
    placed = lax.all_to_all(slotted, ("chan", "x"), split_axis=0, concat_axis=0, tiled=True)
    packed = pl.pallas_call(
        pack_kernel,
        out_shape=jax.ShapeDtypeStruct((GROUPS, BUNDLE, LANES), bf16),
        in_specs=[vmem],
        out_specs=vmem,
        compiler_params=limit(8),
        name="pack",
    )(placed)
    own = lax.all_to_all(packed, ("zh", "zl"), split_axis=0, concat_axis=0, tiled=True)
    other = lax.ppermute(own[:, :EXTRA], "inp", [(0, 1), (1, 0)])
    depth = GROUPS * 64
    left, ring = pl.pallas_call(
        own_kernel,
        out_shape=(jax.ShapeDtypeStruct((512, depth), bf16), jax.ShapeDtypeStruct((512, 10 * LANES), bf16)),
        in_specs=[vmem],
        out_specs=(vmem, vmem),
        compiler_params=limit(8),
        cost_estimate=pl.CostEstimate(flops=2 * 512 * 512 * 512, bytes_accessed=3 * 2**20, transcendentals=0),
        name="own",
    )(own)
    rows, _ = pl.pallas_call(
        other_kernel,
        out_shape=(
            jax.ShapeDtypeStruct((8, PARCEL, LANES), bf16),
            jax.ShapeDtypeStruct((512, 10 * LANES), bf16),
        ),
        in_specs=[vmem, vmem, vmem],
        out_specs=(vmem, vmem),
        input_output_aliases={1: 1},
        compiler_params=limit(12),
        name="other",
    )(left, ring, other)
    parts = lax.all_to_all(rows, ("zl", "x"), split_axis=0, concat_axis=0, tiled=True)
    tiles = pl.pallas_call(
        tiles_kernel,
        out_shape=jax.ShapeDtypeStruct((OWNER_SLOTS, 64, KT * BLK), f32),
        in_specs=[vmem],
        out_specs=hbm,
        scratch_shapes=[VMEM((OWNER_SLOTS, 64, KT * BLK), f32), pltpu.SemaphoreType.DMA((OWNER_SLOTS,))],
        compiler_params=limit(8),
        name="tiles",
    )(parts)
    return tiles.reshape(OWNER_SLOTS, 1, 2, BLK, KT * BLK)


def solution(mesh):
    parts = Mesh(mesh.devices.reshape(2, 8, 4, 2, 4), ("inp", "chan", "zh", "zl", "x"))
    return jax.shard_map(
        on_device,
        mesh=parts,
        in_specs=(P(("inp", "chan"), ("zh", "zl", "x")), P(("inp", "chan"), None), P()),
        out_specs=P("chan", ("inp", "zh", "zl", "x"), None, None, None),
        check_vma=False,
    )
```
